256 devices in a mesh: tm: 64 (over z, y, core), heads: 4 (over x).
Axes of the slice: x: 4, y: 4, z: 8, core: 2. Of those that a mesh axis runs over, the one named last changes fastest.
Arguments:
- video: bfloat16 [128, 196, 768], P('tm'), may hold values from -12 to 12
- t_gain: float32 [768], replicated, may hold values from 0.1 to 1.9
- t_qkv: bfloat16 [3, 768, 768], P(None, 'heads'), may hold values from -3 to 3
- t_out: bfloat16 [768, 768], P('heads'), may hold values from -0.21875 to 0.21875
- s_gain: float32 [768], replicated, may hold values from 0.1 to 1.9
- s_qkv: bfloat16 [3, 768, 768], P(None, 'heads'), may hold values from -3 to 3
- s_out: bfloat16 [768, 768], P('heads'), may hold values from -0.21875 to 0.21875
- m_gain: float32 [768], replicated, may hold values from 0.1 to 1.9
- m_up: bfloat16 [768, 3072], P(None, 'heads'), may hold values from -0.21875 to 0.21875
- m_down: bfloat16 [3072, 768], P('heads'), may hold values from -0.109375 to 0.109375
- m_merge: bfloat16 [3, 768, 768], replicated, may hold values from -0.125 to 0.125
Outputs:
- block_out: bfloat16 [128, 196, 768], P('tm', 'heads')
- merged: bfloat16 [64, 196, 768], P('tm', 'heads')
The draws below stay inside these ranges and needn't reach their ends.
All inputs are finite; a program needn't handle non-finite values.
Results may differ from the reference program's by a relative error of at most 0.02.
Values may be sent and summed in bfloat16 or wider, within the bound.
A program may use at most 64 MiB of HBM per device.

```python
import math
import jax
import jax.numpy as jnp
from jax import lax

D = 768
H = 12
HD = 64
FF = 3072
P_SIZE = 196
F = 128


def drawn_weights(key):
    values = jax.random.normal(key, (3, D, D), jnp.float32) / math.sqrt(D)
    return jnp.clip(values, -3.0, 3.0).astype(jnp.bfloat16)


def draw_t_qkv(key, part):
    key = jax.random.fold_in(key, 11)
    return drawn_weights(key)


def draw_s_qkv(key, part):
    key = jax.random.fold_in(key, 23)
    return drawn_weights(key)


def draw_video(key, part):
    key = jax.random.fold_in(key, 5)
    first, second = jax.random.split(key, 2)
    common = jax.random.normal(first, (P_SIZE, D), jnp.float32)
    noise = jax.random.normal(second, (F, P_SIZE, D), jnp.float32)
    values = 0.7 * common[None] + noise
    return jnp.clip(values, -12.0, 12.0).astype(jnp.bfloat16)


def shard_levels(rng, extent, cuts, low, high):
    factor_of = 1.0
    for axis_at, shards_of in cuts:
        heights = jax.random.uniform(jax.random.fold_in(jax.random.fold_in(rng, 6), axis_at), (shards_of,), jnp.float32, low / len(cuts), high / len(cuts))
        factor_of = factor_of * jnp.repeat(jnp.exp(heights), extent[axis_at] // shards_of).reshape((-1,) + (1,) * (len(extent) - 1 - axis_at))
    return factor_of


def normal_values(own_key, extent, scale, most, pieces=(), dtype=jnp.bfloat16):
    result = scale * jax.random.normal(own_key, extent, jnp.float32)
    if pieces:
        result = result * shard_levels(own_key, extent, pieces, -0.22, 0.18)
    return jnp.clip(result, -most, most).astype(dtype)


def setup_inputs(seed: int = 0) -> dict:
    key_list = jax.random.split(jax.random.key(seed), 12)
    video = draw_video(jax.random.fold_in(key_list[11], 71), 0)
    t_gain = jnp.clip(1.0 + 0.18 * jax.random.normal(key_list[1], (D,), jnp.float32), 0.1, 1.9)
    t_qkv = draw_t_qkv(jax.random.fold_in(key_list[11], 71), 0)
    t_out = normal_values(key_list[3], (D, D), D ** -0.5, 0.21875, ((0, 4),))
    s_gain = jnp.clip(1.0 + 0.18 * jax.random.normal(key_list[4], (D,), jnp.float32), 0.1, 1.9)
    s_qkv = draw_s_qkv(jax.random.fold_in(key_list[11], 71), 0)
    s_out = normal_values(key_list[6], (D, D), D ** -0.5, 0.21875, ((0, 4),))
    m_gain = jnp.clip(1.0 + 0.18 * jax.random.normal(key_list[7], (D,), jnp.float32), 0.1, 1.9)
    m_up = normal_values(key_list[8], (D, FF), D ** -0.5, 0.21875, ((1, 4),))
    m_down = normal_values(key_list[9], (FF, D), FF ** -0.5, 0.109375, ((0, 4),))
    m_merge = normal_values(key_list[10], (3, D, D), (3 * D) ** -0.5, 0.125)
    return {"video": video, "t_gain": t_gain, "t_qkv": t_qkv, "t_out": t_out, "s_gain": s_gain, "s_qkv": s_qkv, "s_out": s_out, "m_gain": m_gain, "m_up": m_up, "m_down": m_down, "m_merge": m_merge}


def layer_norm(values, gain):
    floats = values.astype(jnp.float32)
    centre = lax.optimization_barrier(jnp.mean(floats, axis=-1, keepdims=True))
    spread = lax.optimization_barrier(jnp.mean((floats - centre) ** 2, axis=-1, keepdims=True))
    return (floats - centre) * lax.rsqrt(spread + 1e-06) * gain

def project(rows, matrix):
    return jnp.dot(rows, matrix.T, preferred_element_type=jnp.float32).astype(jnp.bfloat16)

def temporal_one(blocks):
    query_rows, key_rows, value_rows = blocks
    scores = jnp.einsum('fhd,ghd->hfg', query_rows.astype(jnp.float32), key_rows.astype(jnp.float32)) * HD ** (-0.5)
    weights = jax.nn.softmax(scores, axis=-1).astype(jnp.bfloat16)
    return jnp.einsum('hfg,ghd->fhd', weights.astype(jnp.float32), value_rows.astype(jnp.float32)).astype(jnp.bfloat16)

def spatial_one(blocks):
    query_rows, key_rows, value_rows = blocks
    scores = jnp.einsum('phd,rhd->hpr', query_rows.astype(jnp.float32), key_rows.astype(jnp.float32)) * HD ** (-0.5)
    weights = jax.nn.softmax(scores, axis=-1).astype(jnp.bfloat16)
    return jnp.einsum('hpr,rhd->phd', weights.astype(jnp.float32), value_rows.astype(jnp.float32)).astype(jnp.bfloat16)

def reference(video, t_gain, t_qkv, t_out, s_gain, s_qkv, s_out, m_gain, m_up, m_down, m_merge):
    normed = layer_norm(video, t_gain).astype(jnp.bfloat16).reshape(F * P_SIZE, D)
    query_rows = project(normed, t_qkv[0]).reshape(F, P_SIZE, H, HD).transpose(1, 0, 2, 3)
    key_rows = project(normed, t_qkv[1]).reshape(F, P_SIZE, H, HD).transpose(1, 0, 2, 3)
    value_rows = project(normed, t_qkv[2]).reshape(F, P_SIZE, H, HD).transpose(1, 0, 2, 3)
    mixed = lax.map(temporal_one, (query_rows, key_rows, value_rows))
    mixed = mixed.transpose(1, 0, 2, 3).reshape(F * P_SIZE, D)
    after_time = (video.astype(jnp.float32) + jnp.dot(mixed, t_out, preferred_element_type=jnp.float32).reshape(F, P_SIZE, D)).astype(jnp.bfloat16)
    normed = layer_norm(after_time, s_gain).astype(jnp.bfloat16).reshape(F * P_SIZE, D)
    query_rows = project(normed, s_qkv[0]).reshape(F, P_SIZE, H, HD)
    key_rows = project(normed, s_qkv[1]).reshape(F, P_SIZE, H, HD)
    value_rows = project(normed, s_qkv[2]).reshape(F, P_SIZE, H, HD)
    mixed = lax.map(spatial_one, (query_rows, key_rows, value_rows)).reshape(F * P_SIZE, D)
    after_space = (after_time.astype(jnp.float32) + jnp.dot(mixed, s_out, preferred_element_type=jnp.float32).reshape(F, P_SIZE, D)).astype(jnp.bfloat16)
    normed = layer_norm(after_space, m_gain).astype(jnp.bfloat16).reshape(F * P_SIZE, D)
    hidden = jax.nn.gelu(jnp.dot(normed, m_up, preferred_element_type=jnp.float32), approximate=False).astype(jnp.bfloat16)
    block_out = (after_space.astype(jnp.float32) + jnp.dot(hidden, m_down, preferred_element_type=jnp.float32).reshape(F, P_SIZE, D)).astype(jnp.bfloat16)
    extended = jnp.concatenate([jnp.zeros((1, P_SIZE, D), jnp.bfloat16), block_out], axis=0)
    merge_sum = jnp.zeros((F // 2 * P_SIZE, D), jnp.float32)
    for offset in range(3):
        picked = extended[offset:offset + F:2].reshape(F // 2 * P_SIZE, D)
        merge_sum = merge_sum + jnp.dot(picked, m_merge[offset], preferred_element_type=jnp.float32)
    merged = merge_sum.reshape(F // 2, P_SIZE, D).astype(jnp.bfloat16)
    return (block_out, merged)
```

```python
import jax
import jax.numpy as jnp
from jax import lax
from jax.experimental import pallas as pl
from jax.experimental.pallas import tpu as pltpu
from jax.sharding import PartitionSpec as P

HD = 64
MESH = pl.DeviceIdType.MESH
F32 = jnp.float32
BF16 = jnp.bfloat16


def layer_norm(floats, gain):
    centre = jnp.mean(floats, axis=-1, keepdims=True)
    moved = floats - centre
    spread = jnp.mean(moved * moved, axis=-1, keepdims=True)
    return (moved * lax.rsqrt(spread + 1e-06) * gain).astype(BF16)


def dot(a, b):
    return jnp.dot(a, b, preferred_element_type=F32)


def dot_t(a, b):
    return lax.dot_general(a, b, (((1,), (1,)), ((), ())), preferred_element_type=F32)


def iota(shape, axis):
    return lax.broadcasted_iota(jnp.int32, shape, axis)


def attend(queries, keys, values, valid):
    scores = dot_t(queries, keys) * (HD ** -0.5)
    if valid is not None:
        scores = jnp.where(valid, scores, -jnp.inf)
    raised = jnp.exp(scores - jnp.max(scores, axis=-1, keepdims=True))
    total = jnp.sum(raised, axis=-1, keepdims=True)
    return dot(raised.astype(BF16), values) / total


def kernel(
    video, t_gain, t_qkv, t_out, s_gain, s_qkv, s_out, m_gain, m_up, m_down, m_merge,
    block_out, merged,
    vid, w_tqkv, w_tout, w_sqkv, w_sout, w_up, w_down, w_merge,
    fsend, frecv, frecv_extra, rsend, rsend_extra, rrecv,
    hbuf, sqkv, smix, mix_send, mix_recv, gbuf, psend, precv, edge_send, edge_recv,
    load_sem, wt_send, wt_recv, ws_send, ws_recv,
    f_sem, r_sem, h_send, h_recv, x_send, x_recv, g_send, g_recv, p_send, p_recv, e_sem,
):
    tm = lax.axis_index("tm")
    hx = lax.axis_index("heads")
    count = lax.axis_size("tm")
    wide = lax.axis_size("heads")
    positions, model = video.shape[1], video.shape[2]
    quarter = positions // wide
    group = count // wide
    width = t_qkv.shape[1]
    heads = width // HD
    home = tm // group
    rank = lax.rem(tm, group)
    last = rank == group - 1
    rows = hbuf.shape[1]
    half = rows // 2

    def peer(step):
        return lax.rem(hx + step, wide)

    loads = []
    for i, (source, target) in enumerate(
        (
            (video, vid), (t_qkv, w_tqkv), (t_out, w_tout.at[hx]), (s_qkv, w_sqkv),
            (s_out, w_sout.at[hx]), (m_up, w_up), (m_down, w_down), (m_merge, w_merge),
        )
    ):
        copy = pltpu.make_async_copy(source, target, load_sem.at[i])
        copy.start()
        loads.append(copy)

    barrier = pltpu.get_barrier_semaphore()

    @pl.loop(1, count)
    def _(step):
        pl.semaphore_signal(
            barrier, inc=1, device_id={"tm": lax.rem(tm + step, count)}, device_id_type=MESH
        )

    for step in range(1, wide):
        pl.semaphore_signal(
            barrier, inc=1, device_id={"heads": peer(step)}, device_id_type=MESH
        )

    loads[0].wait()
    loads[1].wait()
    tqkv = w_tqkv[...].reshape(3 * width, model)
    for f in range(2):
        normed = layer_norm(vid[f].astype(F32), t_gain[...])
        fsend[:, f] = dot_t(normed, tqkv).astype(BF16)

    pl.semaphore_wait(barrier, count - 1 + wide - 1)

    def first_position(device):
        return (device // group) * quarter + lax.rem(device, group) * 3

    @pl.loop(1, count)
    def _(step):
        to = lax.rem(tm + step, count)
        start = first_position(to)
        pltpu.make_async_remote_copy(
            fsend.at[pl.ds(start, 3)], frecv.at[tm], f_sem.at[0], f_sem.at[1],
            device_id={"tm": to}, device_id_type=MESH,
        ).start()

        @pl.when(lax.rem(to, group) == group - 1)
        def _():
            pltpu.make_async_remote_copy(
                fsend.at[start + 3], frecv_extra.at[tm], f_sem.at[2], f_sem.at[3],
                device_id={"tm": to}, device_id_type=MESH,
            ).start()

    own_start = first_position(tm)
    pltpu.make_async_copy(fsend.at[pl.ds(own_start, 3)], frecv.at[tm], f_sem.at[1]).start()

    @pl.when(last)
    def _():
        pltpu.make_async_copy(fsend.at[own_start + 3], frecv_extra.at[tm], f_sem.at[3]).start()

    gathers = []
    for source, target, send, recv in (
        (t_out, w_tout, wt_send, wt_recv), (s_out, w_sout, ws_send, ws_recv),
    ):
        copies = []
        for step in (1, 3, 2):
            copy = pltpu.make_async_remote_copy(
                source, target.at[hx], send.at[step], recv.at[step],
                device_id={"heads": peer(step)}, device_id_type=MESH,
            )
            copy.start()
            copies.append(copy)
        gathers.append(copies)

    row = iota((rows, positions), 0)
    column = iota((rows, positions), 1)
    place = lax.rem(row, half)
    own_video = jnp.zeros((rows, model), F32)
    for f in range(2):
        pick = (row // half == f) & (place < quarter) & (column == hx * quarter + place)
        own_video += dot(pick.astype(BF16), vid[f])

    pltpu.make_async_copy(frecv, frecv, f_sem.at[1]).wait()

    def temporal(block):
        parts = []
        for head in range(heads):
            at = head * HD
            parts.append(
                attend(
                    block[:, at : at + HD],
                    block[:, width + at : width + at + HD],
                    block[:, 2 * width + at : 2 * width + at + HD],
                    None,
                )
            )
        mixed = jnp.concatenate(parts, axis=1).astype(BF16)
        return mixed.reshape(count, 2, width)

    for p in range(3):
        rsend[:, p] = temporal(frecv[:, p].reshape(2 * count, 3 * width))

    @pl.when(last)
    def _():
        pltpu.make_async_copy(frecv_extra, frecv_extra, f_sem.at[3]).wait()
        rsend_extra[...] = temporal(frecv_extra[...].reshape(2 * count, 3 * width))

    def send_back(to, local):
        pieces = [(rsend.at[to], rrecv.at[hx, pl.ds(3 * rank, 3)], 0, 1)]
        extra = (rsend_extra.at[to], rrecv.at[hx, 3 * group], 2, 3)

        def go(source, target, send, recv):
            if local:
                pltpu.make_async_copy(source, target, r_sem.at[recv]).start()
            else:
                pltpu.make_async_remote_copy(
                    source, target, r_sem.at[send], r_sem.at[recv],
                    device_id={"tm": to, "heads": home}, device_id_type=MESH,
                ).start()

        go(*pieces[0])

        @pl.when(last)
        def _():
            go(*extra)

    @pl.loop(1, count)
    def _(step):
        send_back(lax.rem(tm + step, count), False)

    @pl.when(home == hx)
    def _():
        send_back(tm, True)

    @pl.when(home != hx)
    def _():
        send_back(tm, False)

    pltpu.make_async_copy(
        fsend.at[pl.ds(0, 3 * (count - 1))], fsend.at[pl.ds(0, 3 * (count - 1))], f_sem.at[0]
    ).wait()

    @pl.when(last)
    def _():
        part = fsend.at[pl.ds(0, wide - 1)]
        pltpu.make_async_copy(part, part, f_sem.at[2]).wait()

    @pl.when(jnp.logical_not(last))
    def _():
        part = fsend.at[pl.ds(0, wide)]
        pltpu.make_async_copy(part, part, f_sem.at[2]).wait()

    loads[2].wait()
    for copy in gathers[0]:
        copy.wait()
    row = iota((rows, 2 * quarter), 0)
    column = iota((rows, 2 * quarter), 1)
    place = lax.rem(row, half)
    order = ((place < quarter) & (column == 2 * place + row // half)).astype(BF16)

    most = rrecv.at[:, pl.ds(0, 3 * group)]
    pltpu.make_async_copy(most, most, r_sem.at[1]).wait()
    rest = rrecv.at[:, 3 * group]
    pltpu.make_async_copy(rest, rest, r_sem.at[3]).wait()
    total = own_video
    for x in range(wide):
        mixed = dot(order, rrecv[x].reshape(2 * quarter, width)).astype(BF16)
        total += dot(mixed, w_tout[x])
    x1 = total.astype(BF16).astype(F32)

    def gather(buffer, send, recv):
        copies = {}
        for step in (1, 3, 2):
            copies[step] = pltpu.make_async_remote_copy(
                buffer.at[hx], buffer.at[hx], send.at[step], recv.at[step],
                device_id={"heads": peer(step)}, device_id_type=MESH,
            )
            copies[step].start()
        return copies

    hbuf[hx] = layer_norm(x1, s_gain[...])
    copies = gather(hbuf, h_send, h_recv)
    loads[3].wait()
    for step in (0, 1, 3, 2):
        if step:
            copies[step].wait_recv()
        at = peer(wide - step)
        projected = dot_t(hbuf[at], w_sqkv[...].reshape(3 * width, model))
        for f in range(2):
            sqkv[f, at] = projected[f * half : (f + 1) * half]
    keep = lax.rem(iota((1, wide * half), 1), half) < quarter
    for f in range(2):
        block = sqkv[f].reshape(wide * half, 3 * width).astype(BF16)
        for head in range(heads):
            at = head * HD
            smix[:, f, :, at : at + HD] = attend(
                block[:, at : at + HD],
                block[:, width + at : width + at + HD],
                block[:, 2 * width + at : 2 * width + at + HD],
                keep,
            ).reshape(wide, half, HD)
    mix_send[...] = smix[...].reshape(wide, rows, width).astype(BF16)
    mix_copies = []
    for step in (2, 1, 3):
        copy = pltpu.make_async_remote_copy(
            mix_send.at[peer(step)], mix_recv.at[hx], x_send.at[step], x_recv.at[step],
            device_id={"heads": peer(step)}, device_id_type=MESH,
        )
        copy.start()
        mix_copies.append(copy)
    loads[4].wait()
    for copy in gathers[1]:
        copy.wait()
    total = x1 + dot(mix_send[hx], w_sout[hx])
    for step, copy in zip((2, 1, 3), mix_copies):
        copy.wait_recv()
        at = peer(wide - step)
        total += dot(mix_recv[at], w_sout[at])
    x2 = total.astype(BF16).astype(F32)

    gbuf[hx] = layer_norm(x2, m_gain[...])
    g_copies = gather(gbuf, g_send, g_recv)
    loads[5].wait()
    loads[6].wait()
    p_copies = []
    own_part = None
    for step in (0, 1, 3, 2):
        if step:
            g_copies[step].wait_recv()
        at = peer(wide - step)
        up = dot(gbuf[at], w_up[...])
        hidden = (0.5 * up * (1.0 + lax.erf(up * (0.5 ** 0.5)))).astype(BF16)
        part = dot(hidden, w_down[...])
        if step:
            psend[at] = part.astype(BF16)
            copy = pltpu.make_async_remote_copy(
                psend.at[at], precv.at[hx], p_send.at[step], p_recv.at[step],
                device_id={"heads": at}, device_id_type=MESH,
            )
            copy.start()
            p_copies.append((step, copy))
        else:
            own_part = part
    total = x2 + own_part
    for step, copy in p_copies:
        copy.wait_recv()
        total += precv[peer(step)].astype(F32)
    for f in range(2):
        block_out[f] = total[f * half : f * half + quarter].astype(BF16)
    first = total[:half].astype(BF16)
    second = total[half:].astype(BF16)

    edge_send[0:half] = second
    edge_send[half:] = jnp.zeros((edge_send.shape[0] - half, model), BF16)
    to_next = pltpu.make_async_remote_copy(
        edge_send, edge_recv, e_sem.at[0], e_sem.at[1],
        device_id={"tm": lax.rem(tm + 1, count)}, device_id_type=MESH,
    )

    @pl.when(tm < count - 1)
    def _():
        to_next.start()

    loads[7].wait()
    result = dot(first, w_merge[1]) + dot(second, w_merge[2])

    @pl.when(tm > 0)
    def _():
        to_next.wait_recv()

    @pl.when(tm == 0)
    def _():
        edge_recv[...] = jnp.zeros_like(edge_recv)

    result += dot(edge_recv[0:half], w_merge[0])
    merged[0] = result[:quarter].astype(BF16)

    @pl.when(tm < count - 1)
    def _():
        to_next.wait_send()

    @pl.when(home == hx)
    def _():
        part = rsend.at[pl.ds(0, count - 1)]
        pltpu.make_async_copy(part, part, r_sem.at[0]).wait()

        @pl.when(last)
        def _():
            part = rsend_extra.at[pl.ds(0, count - 1)]
            pltpu.make_async_copy(part, part, r_sem.at[2]).wait()

    @pl.when(home != hx)
    def _():
        pltpu.make_async_copy(rsend, rsend, r_sem.at[0]).wait()

        @pl.when(last)
        def _():
            pltpu.make_async_copy(rsend_extra, rsend_extra, r_sem.at[2]).wait()

    for step in (1, 2, 3):
        copies[step].wait_send()
        g_copies[step].wait_send()
    for copy in mix_copies:
        copy.wait_send()
    for _, copy in p_copies:
        copy.wait_send()


def local(video, t_gain, t_qkv, t_out, s_gain, s_qkv, s_out, m_gain, m_up, m_down, m_merge):
    count = lax.axis_size("tm")
    wide = lax.axis_size("heads")
    frames, positions, model = video.shape
    width = t_qkv.shape[1]
    hidden = m_up.shape[1]
    quarter = positions // wide
    half = -(-quarter // 8) * 8
    rows = 2 * half
    edge = -(-half // 16) * 16
    vmem = pltpu.VMEM
    dma = pltpu.SemaphoreType.DMA
    in_vmem = pl.BlockSpec(memory_space=pltpu.VMEM)
    anywhere = pl.BlockSpec(memory_space=pl.ANY)
    return pl.pallas_call(
        kernel,
        out_shape=(
            jax.ShapeDtypeStruct((frames, quarter, model), BF16),
            jax.ShapeDtypeStruct((frames // 2, quarter, model), BF16),
        ),
        in_specs=[
            anywhere, in_vmem, anywhere, anywhere, in_vmem, anywhere, anywhere, in_vmem,
            anywhere, anywhere, anywhere,
        ],
        out_specs=(in_vmem, in_vmem),
        scratch_shapes=[
            vmem((frames, positions, model), BF16),
            vmem((3, width, model), BF16),
            vmem((wide, width, model), BF16),
            vmem((3, width, model), BF16),
            vmem((wide, width, model), BF16),
            vmem((model, hidden), BF16),
            vmem((hidden, model), BF16),
            vmem((3, model, model), BF16),
            vmem((positions, 2, 3 * width), BF16),
            vmem((count, 3, 2, 3 * width), BF16),
            vmem((count, 2, 3 * width), BF16),
            vmem((count, 3, 2, width), BF16),
            vmem((count, 2, width), BF16),
            vmem((wide, quarter, 2, width), BF16),
            vmem((wide, rows, model), BF16),
            vmem((2, wide, half, 3 * width), F32),
            vmem((wide, 2, half, width), F32),
            vmem((wide, rows, width), BF16),
            vmem((wide, rows, width), BF16),
            vmem((wide, rows, model), BF16),
            vmem((wide, rows, model), BF16),
            vmem((wide, rows, model), BF16),
            vmem((edge, model), BF16),
            vmem((edge, model), BF16),
            dma((8,)), dma((4,)), dma((4,)), dma((4,)), dma((4,)),
            dma((4,)), dma((4,)), dma((4,)), dma((4,)), dma((4,)), dma((4,)),
            dma((4,)), dma((4,)), dma((4,)), dma((4,)), dma((2,)),
        ],
        compiler_params=pltpu.CompilerParams(
            collective_id=0, has_side_effects=True, vmem_limit_bytes=50 * 2**20
        ),
    )(
        video, t_gain[None], t_qkv, t_out, s_gain[None], s_qkv, s_out, m_gain[None],
        m_up, m_down, m_merge,
    )


def solution(mesh):
    placed = (
        P("tm", None, None),
        P(),
        P(None, "heads", None),
        P("heads", None),
        P(),
        P(None, "heads", None),
        P("heads", None),
        P(),
        P(None, "heads"),
        P("heads", None),
        P(),
    )
    return jax.shard_map(
        local,
        mesh=mesh,
        in_specs=placed,
        out_specs=(P("tm", "heads", None), P("tm", "heads", None)),
        check_vma=False,
    )
```

```python
import jax
import jax.numpy as jnp
from jax import lax
from jax.experimental import pallas as pl
from jax.experimental.pallas import tpu as pltpu
from jax.sharding import PartitionSpec as P

HD = 64
MESH = pl.DeviceIdType.MESH
F32 = jnp.float32
BF16 = jnp.bfloat16


def layer_norm(floats, gain):
    centre = jnp.mean(floats, axis=-1, keepdims=True)
    moved = floats - centre
    spread = jnp.mean(moved * moved, axis=-1, keepdims=True)
    return (moved * lax.rsqrt(spread + 1e-06) * gain).astype(BF16)


def dot(a, b):
    return jnp.dot(a, b, preferred_element_type=F32)


def dot_t(a, b):
    return lax.dot_general(a, b, (((1,), (1,)), ((), ())), preferred_element_type=F32)


def iota(shape, axis):
    return lax.broadcasted_iota(jnp.int32, shape, axis)


def attend(queries, keys, values, valid):
    scores = dot_t(queries, keys) * (HD ** -0.5)
    if valid is not None:
        scores = jnp.where(valid, scores, -jnp.inf)
    raised = jnp.exp(scores - jnp.max(scores, axis=-1, keepdims=True))
    total = jnp.sum(raised, axis=-1, keepdims=True)
    return dot(raised.astype(BF16), values) / total


def kernel(
    video, t_gain, t_qkv, t_out, s_gain, s_qkv, s_out, m_gain, m_up, m_down, m_merge,
    block_out, merged,
    vid, w_tqkv, w_tout, w_sqkv, w_sout, w_up, w_down, w_merge,
    fsend, frecv, frecv_extra, rsend, rsend_extra, rrecv,
    hbuf, sqkv, smix, mix_send, mix_recv, gbuf, psend, precv, edge_send, edge_recv,
    load_sem, wt_send, wt_recv, ws_send, ws_recv,
    f_sem, r_sem, h_send, h_recv, x_send, x_recv, g_send, g_recv, p_send, p_recv, e_sem,
):
    tm = lax.axis_index("tm")
    hx = lax.axis_index("heads")
    count = lax.axis_size("tm")
    wide = lax.axis_size("heads")
    positions, model = video.shape[0], video.shape[2]
    quarter = positions // wide
    group = count // wide
    width = t_qkv.shape[1]
    heads = width // HD
    home = tm // group
    rank = lax.rem(tm, group)
    last = rank == group - 1
    rows = hbuf.shape[1]
    half = rows // 2

    def peer(step):
        return lax.rem(hx + step, wide)

    loads = []
    for i, (source, target) in enumerate(
        (
            (video, vid), (t_qkv, w_tqkv), (t_out, w_tout.at[hx]), (s_qkv, w_sqkv),
            (s_out, w_sout.at[hx]), (m_up, w_up), (m_down, w_down), (m_merge, w_merge),
        )
    ):
        copy = pltpu.make_async_copy(source, target, load_sem.at[i])
        copy.start()
        loads.append(copy)

    barrier = pltpu.get_barrier_semaphore()

    def other(k):
        side = lax.rem(k, 2)
        return lax.rem(tm + count // 2 + (1 - 2 * side) * ((k + side) // 2) + count, count)

    @pl.loop(0, count - 1)
    def _(k):
        pl.semaphore_signal(barrier, inc=1, device_id={"tm": other(k)}, device_id_type=MESH)

    for step in range(1, wide):
        pl.semaphore_signal(
            barrier, inc=1, device_id={"heads": peer(step)}, device_id_type=MESH
        )

    loads[0].wait()
    loads[1].wait()
    tqkv = w_tqkv[...].reshape(3 * width, model)
    normed = layer_norm(vid[...].reshape(2 * positions, model).astype(F32), t_gain[...])
    fsend[...] = dot_t(normed, tqkv).astype(BF16).reshape(positions, 2, 3 * width)

    pl.semaphore_wait(barrier, count - 1 + wide - 1)

    def first_position(device):
        return (device // group) * quarter + lax.rem(device, group) * 3

    @pl.loop(0, count - 1)
    def _(k):
        to = other(k)
        start = first_position(to)
        pltpu.make_async_remote_copy(
            fsend.at[pl.ds(start, 3)], frecv.at[tm], f_sem.at[0], f_sem.at[1],
            device_id={"tm": to}, device_id_type=MESH,
        ).start()

        @pl.when(lax.rem(to, group) == group - 1)
        def _():
            pltpu.make_async_remote_copy(
                fsend.at[start + 3], frecv_extra.at[tm], f_sem.at[2], f_sem.at[3],
                device_id={"tm": to}, device_id_type=MESH,
            ).start()

    own_start = first_position(tm)
    pltpu.make_async_copy(fsend.at[pl.ds(own_start, 3)], frecv.at[tm], f_sem.at[1]).start()

    @pl.when(last)
    def _():
        pltpu.make_async_copy(fsend.at[own_start + 3], frecv_extra.at[tm], f_sem.at[3]).start()

    gathers = []
    for source, target, send, recv in (
        (t_out, w_tout, wt_send, wt_recv), (s_out, w_sout, ws_send, ws_recv),
    ):
        copies = []
        for step in (1, 3, 2):
            copy = pltpu.make_async_remote_copy(
                source, target.at[hx], send.at[step], recv.at[step],
                device_id={"heads": peer(step)}, device_id_type=MESH,
            )
            copy.start()
            copies.append(copy)
        gathers.append(copies)

    row = iota((rows, 2 * quarter), 0)
    column = iota((rows, 2 * quarter), 1)
    place = lax.rem(row, half)
    order = ((place < quarter) & (column == 2 * place + row // half)).astype(BF16)
    own_video = dot(order, vid[pl.ds(hx * quarter, quarter)].reshape(2 * quarter, model))

    pltpu.make_async_copy(frecv, frecv, f_sem.at[1]).wait()

    def temporal(block):
        parts = []
        for head in range(heads):
            at = head * HD
            parts.append(
                attend(
                    block[:, at : at + HD],
                    block[:, width + at : width + at + HD],
                    block[:, 2 * width + at : 2 * width + at + HD],
                    None,
                )
            )
        mixed = jnp.concatenate(parts, axis=1).astype(BF16)
        return mixed.reshape(count, 2, width)

    for p in range(3):
        rsend[:, p] = temporal(frecv[:, p].reshape(2 * count, 3 * width))

    @pl.when(last)
    def _():
        pltpu.make_async_copy(frecv_extra, frecv_extra, f_sem.at[3]).wait()
        rsend_extra[...] = temporal(frecv_extra[...].reshape(2 * count, 3 * width))

    def send_back(to, local):
        pieces = [(rsend.at[to], rrecv.at[hx, pl.ds(3 * rank, 3)], 0, 1)]
        extra = (rsend_extra.at[to], rrecv.at[hx, 3 * group], 2, 3)

        def go(source, target, send, recv):
            if local:
                pltpu.make_async_copy(source, target, r_sem.at[recv]).start()
            else:
                pltpu.make_async_remote_copy(
                    source, target, r_sem.at[send], r_sem.at[recv],
                    device_id={"tm": to, "heads": home}, device_id_type=MESH,
                ).start()

        go(*pieces[0])

        @pl.when(last)
        def _():
            go(*extra)

    @pl.loop(0, count - 1)
    def _(k):
        send_back(other(k), False)

    @pl.when(home == hx)
    def _():
        send_back(tm, True)

    @pl.when(home != hx)
    def _():
        send_back(tm, False)

    pltpu.make_async_copy(
        fsend.at[pl.ds(0, 3 * (count - 1))], fsend.at[pl.ds(0, 3 * (count - 1))], f_sem.at[0]
    ).wait()

    @pl.when(last)
    def _():
        part = fsend.at[pl.ds(0, wide - 1)]
        pltpu.make_async_copy(part, part, f_sem.at[2]).wait()

    @pl.when(jnp.logical_not(last))
    def _():
        part = fsend.at[pl.ds(0, wide)]
        pltpu.make_async_copy(part, part, f_sem.at[2]).wait()

    loads[2].wait()
    for copy in gathers[0]:
        copy.wait()
    most = rrecv.at[:, pl.ds(0, 3 * group)]
    pltpu.make_async_copy(most, most, r_sem.at[1]).wait()
    rest = rrecv.at[:, 3 * group]
    pltpu.make_async_copy(rest, rest, r_sem.at[3]).wait()
    total = own_video
    for x in range(wide):
        mixed = dot(order, rrecv[x].reshape(2 * quarter, width)).astype(BF16)
        total += dot(mixed, w_tout[x])
    x1 = total.astype(BF16).astype(F32)

    def gather(buffer, send, recv):
        copies = {}
        for step in (1, 3, 2):
            copies[step] = pltpu.make_async_remote_copy(
                buffer.at[hx], buffer.at[hx], send.at[step], recv.at[step],
                device_id={"heads": peer(step)}, device_id_type=MESH,
            )
            copies[step].start()
        return copies

    hbuf[hx] = layer_norm(x1, s_gain[...])
    copies = gather(hbuf, h_send, h_recv)
    loads[3].wait()
    for step in (0, 1, 3, 2):
        if step:
            copies[step].wait_recv()
        at = peer(wide - step)
        projected = dot_t(hbuf[at], w_sqkv[...].reshape(3 * width, model))
        for f in range(2):
            sqkv[f, at] = projected[f * half : (f + 1) * half]
    keep = lax.rem(iota((1, wide * half), 1), half) < quarter
    for f in range(2):
        block = sqkv[f].reshape(wide * half, 3 * width).astype(BF16)
        for head in range(heads):
            at = head * HD
            smix[:, f, :, at : at + HD] = attend(
                block[:, at : at + HD],
                block[:, width + at : width + at + HD],
                block[:, 2 * width + at : 2 * width + at + HD],
                keep,
            ).reshape(wide, half, HD)
    mix_send[...] = smix[...].reshape(wide, rows, width).astype(BF16)
    mix_copies = []
    for step in (2, 1, 3):
        copy = pltpu.make_async_remote_copy(
            mix_send.at[peer(step)], mix_recv.at[hx], x_send.at[step], x_recv.at[step],
            device_id={"heads": peer(step)}, device_id_type=MESH,
        )
        copy.start()
        mix_copies.append(copy)
    loads[4].wait()
    for copy in gathers[1]:
        copy.wait()
    total = x1 + dot(mix_send[hx], w_sout[hx])
    for step, copy in zip((2, 1, 3), mix_copies):
        copy.wait_recv()
        at = peer(wide - step)
        total += dot(mix_recv[at], w_sout[at])
    x2 = total.astype(BF16).astype(F32)

    gbuf[hx] = layer_norm(x2, m_gain[...])
    g_copies = gather(gbuf, g_send, g_recv)
    loads[5].wait()
    loads[6].wait()
    p_copies = []
    own_part = None
    for step in (0, 1, 3, 2):
        if step:
            g_copies[step].wait_recv()
        at = peer(wide - step)
        up = dot(gbuf[at], w_up[...])
        hidden = (0.5 * up * (1.0 + lax.erf(up * (0.5 ** 0.5)))).astype(BF16)
        part = dot(hidden, w_down[...])
        if step:
            psend[at] = part.astype(BF16)
            copy = pltpu.make_async_remote_copy(
                psend.at[at], precv.at[hx], p_send.at[step], p_recv.at[step],
                device_id={"heads": at}, device_id_type=MESH,
            )
            copy.start()
            p_copies.append((step, copy))
        else:
            own_part = part
    total = x2 + own_part
    for step, copy in p_copies:
        copy.wait_recv()
        total += precv[peer(step)].astype(F32)
    for f in range(2):
        block_out[:, f] = total[f * half : f * half + quarter].astype(BF16)
    first = total[:half].astype(BF16)
    second = total[half:].astype(BF16)

    edge_send[0:half] = second
    edge_send[half:] = jnp.zeros((edge_send.shape[0] - half, model), BF16)
    to_next = pltpu.make_async_remote_copy(
        edge_send, edge_recv, e_sem.at[0], e_sem.at[1],
        device_id={"tm": lax.rem(tm + 1, count)}, device_id_type=MESH,
    )

    @pl.when(tm < count - 1)
    def _():
        to_next.start()

    loads[7].wait()
    result = dot(first, w_merge[1]) + dot(second, w_merge[2])

    @pl.when(tm > 0)
    def _():
        to_next.wait_recv()

    @pl.when(tm == 0)
    def _():
        edge_recv[...] = jnp.zeros_like(edge_recv)

    result += dot(edge_recv[0:half], w_merge[0])
    merged[0] = result[:quarter].astype(BF16)

    @pl.when(tm < count - 1)
    def _():
        to_next.wait_send()

    @pl.when(home == hx)
    def _():
        part = rsend.at[pl.ds(0, count - 1)]
        pltpu.make_async_copy(part, part, r_sem.at[0]).wait()

        @pl.when(last)
        def _():
            part = rsend_extra.at[pl.ds(0, count - 1)]
            pltpu.make_async_copy(part, part, r_sem.at[2]).wait()

    @pl.when(home != hx)
    def _():
        pltpu.make_async_copy(rsend, rsend, r_sem.at[0]).wait()

        @pl.when(last)
        def _():
            pltpu.make_async_copy(rsend_extra, rsend_extra, r_sem.at[2]).wait()

    for step in (1, 2, 3):
        copies[step].wait_send()
        g_copies[step].wait_send()
    for copy in mix_copies:
        copy.wait_send()
    for _, copy in p_copies:
        copy.wait_send()


def local(video, t_gain, t_qkv, t_out, s_gain, s_qkv, s_out, m_gain, m_up, m_down, m_merge):
    count = lax.axis_size("tm")
    wide = lax.axis_size("heads")
    frames, positions, model = video.shape
    width = t_qkv.shape[1]
    hidden = m_up.shape[1]
    quarter = positions // wide
    half = -(-quarter // 8) * 8
    rows = 2 * half
    edge = -(-half // 16) * 16
    vmem = pltpu.VMEM
    dma = pltpu.SemaphoreType.DMA
    in_vmem = pl.BlockSpec(memory_space=pltpu.VMEM)
    anywhere = pl.BlockSpec(memory_space=pl.ANY)
    out, together = pl.pallas_call(
        kernel,
        out_shape=(
            jax.ShapeDtypeStruct((quarter, frames, model), BF16),
            jax.ShapeDtypeStruct((frames // 2, quarter, model), BF16),
        ),
        in_specs=[
            anywhere, in_vmem, anywhere, anywhere, in_vmem, anywhere, anywhere, in_vmem,
            anywhere, anywhere, anywhere,
        ],
        out_specs=(in_vmem, in_vmem),
        scratch_shapes=[
            vmem((positions, frames, model), BF16),
            vmem((3, width, model), BF16),
            vmem((wide, width, model), BF16),
            vmem((3, width, model), BF16),
            vmem((wide, width, model), BF16),
            vmem((model, hidden), BF16),
            vmem((hidden, model), BF16),
            vmem((3, model, model), BF16),
            vmem((positions, 2, 3 * width), BF16),
            vmem((count, 3, 2, 3 * width), BF16),
            vmem((count, 2, 3 * width), BF16),
            vmem((count, 3, 2, width), BF16),
            vmem((count, 2, width), BF16),
            vmem((wide, quarter, 2, width), BF16),
            vmem((wide, rows, model), BF16),
            vmem((2, wide, half, 3 * width), F32),
            vmem((wide, 2, half, width), F32),
            vmem((wide, rows, width), BF16),
            vmem((wide, rows, width), BF16),
            vmem((wide, rows, model), BF16),
            vmem((wide, rows, model), BF16),
            vmem((wide, rows, model), BF16),
            vmem((edge, model), BF16),
            vmem((edge, model), BF16),
            dma((8,)), dma((4,)), dma((4,)), dma((4,)), dma((4,)),
            dma((4,)), dma((4,)), dma((4,)), dma((4,)), dma((4,)), dma((4,)),
            dma((4,)), dma((4,)), dma((4,)), dma((4,)), dma((2,)),
        ],
        compiler_params=pltpu.CompilerParams(
            collective_id=0, has_side_effects=True, vmem_limit_bytes=60 * 2**20
        ),
    )(
        jnp.swapaxes(video, 0, 1), t_gain, t_qkv, t_out, s_gain, s_qkv, s_out, m_gain,
        m_up, m_down, m_merge,
    )
    return jnp.swapaxes(out, 0, 1), together


def solution(mesh):
    placed = (
        P("tm", None, None),
        P(),
        P(None, "heads", None),
        P("heads", None),
        P(),
        P(None, "heads", None),
        P("heads", None),
        P(),
        P(None, "heads"),
        P("heads", None),
        P(),
    )
    return jax.shard_map(
        local,
        mesh=mesh,
        in_specs=placed,
        out_specs=(P("tm", "heads", None), P("tm", "heads", None)),
        check_vma=False,
    )
```

```python
import jax
import jax.numpy as jnp
from jax import lax
from jax.experimental import pallas as pl
from jax.experimental.pallas import tpu as pltpu
from jax.sharding import PartitionSpec as P

HD = 64
MESH = pl.DeviceIdType.MESH
F32 = jnp.float32
BF16 = jnp.bfloat16


def layer_norm(floats, gain):
    centre = jnp.mean(floats, axis=-1, keepdims=True)
    moved = floats - centre
    spread = jnp.mean(moved * moved, axis=-1, keepdims=True)
    return (moved * lax.rsqrt(spread + 1e-06) * gain).astype(BF16)


def dot(a, b):
    return jnp.dot(a, b, preferred_element_type=F32)


def dot_t(a, b):
    return lax.dot_general(a, b, (((1,), (1,)), ((), ())), preferred_element_type=F32)


def iota(shape, axis):
    return lax.broadcasted_iota(jnp.int32, shape, axis)


def attend(queries, keys, values, valid):
    scores = dot_t(queries, keys) * (HD ** -0.5)
    if valid is not None:
        scores = jnp.where(valid, scores, -jnp.inf)
    raised = jnp.exp(scores - jnp.max(scores, axis=-1, keepdims=True))
    total = jnp.sum(raised, axis=-1, keepdims=True)
    return dot(raised.astype(BF16), values) / total


def kernel(
    video, t_gain, t_qkv, t_out, s_gain, s_qkv, s_out, m_gain, m_up, m_down, m_merge,
    block_out, merged,
    vid, w_tqkv, w_out, w_sqkv, w_mlp, w_merge,
    fsend, frecv, frecv_extra, rsend, rsend_extra, rrecv,
    hbuf, sqkv, smix, mix_send, mix_recv, edge_send, edge_recv,
    load_sem, t_sem, s_sem, w_sem, y_sem, c_sem, f_sem, r_sem, h_sem, x_sem, e_sem,
):
    tm = lax.axis_index("tm")
    hx = lax.axis_index("heads")
    count = lax.axis_size("tm")
    wide = lax.axis_size("heads")
    positions, model = video.shape[0], video.shape[2]
    quarter = positions // wide
    group = count // wide
    width = t_qkv.shape[1]
    heads = width // HD
    home = tm // group
    rank = lax.rem(tm, group)
    last = rank == group - 1
    rows = hbuf.shape[1]
    half = rows // 2

    hidden = m_up.shape[1]
    share = (model + hidden) // 8
    core = lax.rem(tm, 2)
    ring = lax.rem(tm // 2, 4)

    def peer(step):
        return lax.rem(hx + step, wide)

    def along(step):
        return tm // 8 * 8 + lax.rem(ring + step, 4) * 2 + core

    def remote(source, target, sems, i, **to):
        return pltpu.make_async_remote_copy(
            source, target, sems.at[0, i], sems.at[1, i], device_id=to, device_id_type=MESH
        )

    loads = []
    for i, (source, target) in enumerate(
        (
            (video, vid), (t_qkv, w_tqkv), (m_up, w_mlp.at[0, pl.ds(0, model)]),
            (m_down, w_mlp.at[0, pl.ds(model, hidden)]), (t_out, w_out.at[0, pl.ds(0, width)]),
            (s_out, w_out.at[0, pl.ds(width, width)]), (s_qkv, w_sqkv), (m_merge, w_merge),
        )
    ):
        copy = pltpu.make_async_copy(source, target, load_sem.at[i])
        copy.start()
        loads.append(copy)

    barrier = pltpu.get_barrier_semaphore()

    def other(k):
        side = lax.rem(k, 2)
        return lax.rem(tm + count // 2 + (1 - 2 * side) * ((k + side) // 2) + count, count)

    @pl.loop(0, count - 1)
    def _(k):
        pl.semaphore_signal(barrier, inc=1, device_id={"tm": other(k)}, device_id_type=MESH)

    for step in range(1, wide):
        pl.semaphore_signal(
            barrier, inc=1, device_id={"heads": peer(step)}, device_id_type=MESH
        )

    loads[0].wait()
    loads[1].wait()
    tqkv = w_tqkv[...].reshape(3 * width, model)
    normed = layer_norm(vid[...].reshape(2 * positions, model).astype(F32), t_gain[...])
    fsend[...] = dot_t(normed, tqkv).astype(BF16).reshape(positions, 2, 3 * width)

    pl.semaphore_wait(barrier, count - 1 + wide - 1)

    def first_position(device):
        return (device // group) * quarter + lax.rem(device, group) * 3

    @pl.loop(0, count - 1)
    def _(k):
        to = other(k)
        start = first_position(to)
        pltpu.make_async_remote_copy(
            fsend.at[pl.ds(start, 3)], frecv.at[tm], f_sem.at[0], f_sem.at[1],
            device_id={"tm": to}, device_id_type=MESH,
        ).start()

        @pl.when(lax.rem(to, group) == group - 1)
        def _():
            pltpu.make_async_remote_copy(
                fsend.at[start + 3], frecv_extra.at[tm], f_sem.at[2], f_sem.at[3],
                device_id={"tm": to}, device_id_type=MESH,
            ).start()

    own_start = first_position(tm)
    pltpu.make_async_copy(fsend.at[pl.ds(own_start, 3)], frecv.at[tm], f_sem.at[1]).start()

    @pl.when(last)
    def _():
        pltpu.make_async_copy(fsend.at[own_start + 3], frecv_extra.at[tm], f_sem.at[3]).start()

    def rows_of(step):
        return (2 * lax.rem(ring + step, 4) + core) * share

    def piece(step, begin, size):
        start = pl.multiple_of(rows_of(step) + begin, 16)
        return w_mlp.at[pl.ds(1, wide - 1), pl.ds(start, size)]

    def fetch(buffer, start, size, sems):
        start = pl.multiple_of(start, 16)
        copies = []
        for step in (2, 1, 3):
            copy = remote(
                buffer.at[0, pl.ds(start, size)], buffer.at[wide - step, pl.ds(start, size)],
                sems, step, heads=peer(step),
            )
            copy.start()
            copies.append(copy)
        return copies

    def give(block, i):
        copy = remote(block, block, c_sem, i, tm=tm + 1 - 2 * core)
        copy.start()
        return copy

    half_width = width // 2
    loads[2].wait()
    loads[3].wait()
    w_copies = fetch(w_mlp, rows_of(0), share, w_sem)
    loads[4].wait()
    t_copies = fetch(w_out, core * half_width, half_width, t_sem)
    loads[5].wait()
    s_copies = fetch(w_out, width + core * half_width, half_width, s_sem)

    row = iota((rows, 2 * quarter), 0)
    column = iota((rows, 2 * quarter), 1)
    place = lax.rem(row, half)
    order = ((place < quarter) & (column == 2 * place + row // half)).astype(BF16)
    own_video = dot(order, vid[pl.ds(hx * quarter, quarter)].reshape(2 * quarter, model))

    pltpu.make_async_copy(frecv, frecv, f_sem.at[1]).wait()

    for copy in w_copies:
        copy.wait_recv()
    part = share // 2
    y_copies = [
        remote(piece(0, 0, part), piece(0, 0, part), y_sem, 0, tm=along(1)),
        remote(piece(0, part, part), piece(0, part, part), y_sem, 1, tm=along(3)),
        remote(piece(0, part, part), piece(0, part, part), y_sem, 2, tm=along(1)),
        remote(piece(0, 0, part), piece(0, 0, part), y_sem, 3, tm=along(3)),
    ]
    for copy in y_copies:
        copy.start()
    given = [give(piece(0, 0, share), 0)]

    def temporal(block):
        parts = []
        for head in range(heads):
            at = head * HD
            parts.append(
                attend(
                    block[:, at : at + HD],
                    block[:, width + at : width + at + HD],
                    block[:, 2 * width + at : 2 * width + at + HD],
                    None,
                )
            )
        mixed = jnp.concatenate(parts, axis=1).astype(BF16)
        return mixed.reshape(count, 2, width)

    for p in range(3):
        rsend[:, p] = temporal(frecv[:, p].reshape(2 * count, 3 * width))

    @pl.when(last)
    def _():
        pltpu.make_async_copy(frecv_extra, frecv_extra, f_sem.at[3]).wait()
        rsend_extra[...] = temporal(frecv_extra[...].reshape(2 * count, 3 * width))

    def send_back(to, local):
        pieces = [(rsend.at[to], rrecv.at[hx, pl.ds(3 * rank, 3)], 0, 1)]
        extra = (rsend_extra.at[to], rrecv.at[hx, 3 * group], 2, 3)

        def go(source, target, send, recv):
            if local:
                pltpu.make_async_copy(source, target, r_sem.at[recv]).start()
            else:
                pltpu.make_async_remote_copy(
                    source, target, r_sem.at[send], r_sem.at[recv],
                    device_id={"tm": to, "heads": home}, device_id_type=MESH,
                ).start()

        go(*pieces[0])

        @pl.when(last)
        def _():
            go(*extra)

    @pl.loop(0, count - 1)
    def _(k):
        send_back(other(k), False)

    @pl.when(home == hx)
    def _():
        send_back(tm, True)

    @pl.when(home != hx)
    def _():
        send_back(tm, False)

    def give_out(copies, start, i):
        for copy in copies:
            copy.wait_recv()
        start = pl.multiple_of(start + core * half_width, 16)
        return give(w_out.at[pl.ds(1, wide - 1), pl.ds(start, half_width)], i)

    given_t = give_out(t_copies, 0, 4)

    pltpu.make_async_copy(
        fsend.at[pl.ds(0, 3 * (count - 1))], fsend.at[pl.ds(0, 3 * (count - 1))], f_sem.at[0]
    ).wait()

    @pl.when(last)
    def _():
        part = fsend.at[pl.ds(0, wide - 1)]
        pltpu.make_async_copy(part, part, f_sem.at[2]).wait()

    @pl.when(jnp.logical_not(last))
    def _():
        part = fsend.at[pl.ds(0, wide)]
        pltpu.make_async_copy(part, part, f_sem.at[2]).wait()

    most = rrecv.at[:, pl.ds(0, 3 * group)]
    pltpu.make_async_copy(most, most, r_sem.at[1]).wait()
    rest = rrecv.at[:, 3 * group]
    pltpu.make_async_copy(rest, rest, r_sem.at[3]).wait()
    y_copies[0].wait_recv()
    y_copies.append(remote(piece(3, 0, part), piece(3, 0, part), y_sem, 4, tm=along(1)))
    y_copies[4].start()
    y_copies[1].wait_recv()
    y_copies.append(remote(piece(1, part, part), piece(1, part, part), y_sem, 5, tm=along(3)))
    y_copies[5].start()
    given_s = give_out(s_copies, width, 5)
    given_t.wait_recv()
    total = own_video
    for slot in range(wide):
        mixed = dot(order, rrecv[peer(slot)].reshape(2 * quarter, width)).astype(BF16)
        total += dot(mixed, w_out[slot, 0:width])
    x1 = total.astype(BF16).astype(F32)

    hbuf[hx] = layer_norm(x1, s_gain[...])
    copies = {}
    for step in (1, 3, 2):
        copies[step] = remote(hbuf.at[hx], hbuf.at[hx], h_sem, step, heads=peer(step))
        copies[step].start()
    loads[6].wait()
    for step in (0, 1, 3, 2):
        if step:
            copies[step].wait_recv()
        at = peer(wide - step)
        projected = dot_t(hbuf[at], w_sqkv[...].reshape(3 * width, model))
        for f in range(2):
            sqkv[f, at] = projected[f * half : (f + 1) * half]
    for copy in y_copies[2:4]:
        copy.wait_recv()
    given.append(give(piece(3, 0, share), 1))
    given.append(give(piece(1, 0, share), 2))
    keep = lax.rem(iota((1, wide * half), 1), half) < quarter
    for f in range(2):
        block = sqkv[f].reshape(wide * half, 3 * width).astype(BF16)
        for head in range(heads):
            at = head * HD
            smix[:, f, :, at : at + HD] = attend(
                block[:, at : at + HD],
                block[:, width + at : width + at + HD],
                block[:, 2 * width + at : 2 * width + at + HD],
                keep,
            ).reshape(wide, half, HD)
    mix_send[...] = smix[...].reshape(wide, rows, width).astype(BF16)
    mix_copies = []
    for step in (2, 1, 3):
        copy = remote(mix_send.at[peer(step)], mix_recv.at[hx], x_sem, step, heads=peer(step))
        copy.start()
        mix_copies.append(copy)
    for copy in y_copies[4:]:
        copy.wait_recv()
    given.append(give(piece(2, 0, share), 3))
    given_s.wait_recv()
    total = x1 + dot(mix_send[hx], w_out[0, width:])
    for step, copy in zip((2, 1, 3), mix_copies):
        copy.wait_recv()
        total += dot(mix_recv[peer(wide - step)], w_out[wide - step, width:])
    x2 = total.astype(BF16).astype(F32)

    normed = layer_norm(x2, m_gain[...])
    total = x2
    for slot in range(wide):
        if slot == 1:
            for copy in given:
                copy.wait_recv()
        up = dot(normed, w_mlp[slot, 0:model])
        shown = (0.5 * up * (1.0 + lax.erf(up * (0.5 ** 0.5)))).astype(BF16)
        total += dot(shown, w_mlp[slot, model:])
    for f in range(2):
        block_out[:, f] = total[f * half : f * half + quarter].astype(BF16)
    first = total[:half].astype(BF16)
    second = total[half:].astype(BF16)

    edge_send[0:half] = second
    edge_send[half:] = jnp.zeros((edge_send.shape[0] - half, model), BF16)
    to_next = pltpu.make_async_remote_copy(
        edge_send, edge_recv, e_sem.at[0], e_sem.at[1],
        device_id={"tm": lax.rem(tm + 1, count)}, device_id_type=MESH,
    )

    @pl.when(tm < count - 1)
    def _():
        to_next.start()

    loads[7].wait()
    result = dot(first, w_merge[1]) + dot(second, w_merge[2])

    @pl.when(tm > 0)
    def _():
        to_next.wait_recv()

    @pl.when(tm == 0)
    def _():
        edge_recv[...] = jnp.zeros_like(edge_recv)

    result += dot(edge_recv[0:half], w_merge[0])
    merged[0] = result[:quarter].astype(BF16)

    @pl.when(tm < count - 1)
    def _():
        to_next.wait_send()

    @pl.when(home == hx)
    def _():
        part = rsend.at[pl.ds(0, count - 1)]
        pltpu.make_async_copy(part, part, r_sem.at[0]).wait()

        @pl.when(last)
        def _():
            part = rsend_extra.at[pl.ds(0, count - 1)]
            pltpu.make_async_copy(part, part, r_sem.at[2]).wait()

    @pl.when(home != hx)
    def _():
        pltpu.make_async_copy(rsend, rsend, r_sem.at[0]).wait()

        @pl.when(last)
        def _():
            pltpu.make_async_copy(rsend_extra, rsend_extra, r_sem.at[2]).wait()

    for copy in (
        *copies.values(), *mix_copies, *w_copies, *t_copies, *s_copies, *y_copies, *given,
        given_t, given_s,
    ):
        copy.wait_send()


def local(video, t_gain, t_qkv, t_out, s_gain, s_qkv, s_out, m_gain, m_up, m_down, m_merge):
    count = lax.axis_size("tm")
    wide = lax.axis_size("heads")
    frames, positions, model = video.shape
    width = t_qkv.shape[1]
    hidden = m_up.shape[1]
    quarter = positions // wide
    half = -(-quarter // 8) * 8
    rows = 2 * half
    edge = -(-half // 16) * 16
    vmem = pltpu.VMEM
    dma = pltpu.SemaphoreType.DMA
    in_vmem = pl.BlockSpec(memory_space=pltpu.VMEM)
    anywhere = pl.BlockSpec(memory_space=pl.ANY)
    out, together = pl.pallas_call(
        kernel,
        out_shape=(
            jax.ShapeDtypeStruct((quarter, frames, model), BF16),
            jax.ShapeDtypeStruct((frames // 2, quarter, model), BF16),
        ),
        in_specs=[
            anywhere, in_vmem, anywhere, anywhere, in_vmem, anywhere, anywhere, in_vmem,
            anywhere, anywhere, anywhere,
        ],
        out_specs=(in_vmem, in_vmem),
        scratch_shapes=[
            vmem((positions, frames, model), BF16),
            vmem((3, width, model), BF16),
            vmem((wide, 2 * width, model), BF16),
            vmem((3, width, model), BF16),
            vmem((wide, model + hidden, model), BF16),
            vmem((3, model, model), BF16),
            vmem((positions, 2, 3 * width), BF16),
            vmem((count, 3, 2, 3 * width), BF16),
            vmem((count, 2, 3 * width), BF16),
            vmem((count, 3, 2, width), BF16),
            vmem((count, 2, width), BF16),
            vmem((wide, quarter, 2, width), BF16),
            vmem((wide, rows, model), BF16),
            vmem((2, wide, half, 3 * width), F32),
            vmem((wide, 2, half, width), F32),
            vmem((wide, rows, width), BF16),
            vmem((wide, rows, width), BF16),
            vmem((edge, model), BF16),
            vmem((edge, model), BF16),
            dma((8,)), dma((2, 4)), dma((2, 4)), dma((2, 4)), dma((2, 6)), dma((2, 6)),
            dma((4,)), dma((4,)), dma((2, 4)), dma((2, 4)), dma((2,)),
        ],
        compiler_params=pltpu.CompilerParams(
            collective_id=0, has_side_effects=True, vmem_limit_bytes=60 * 2**20
        ),
    )(
        jnp.swapaxes(video, 0, 1), t_gain, t_qkv, t_out, s_gain, s_qkv, s_out, m_gain,
        m_up, m_down, m_merge,
    )
    return jnp.swapaxes(out, 0, 1), together


def solution(mesh):
    placed = (
        P("tm", None, None),
        P(),
        P(None, "heads", None),
        P("heads", None),
        P(),
        P(None, "heads", None),
        P("heads", None),
        P(),
        P(None, "heads"),
        P("heads", None),
        P(),
    )
    return jax.shard_map(
        local,
        mesh=mesh,
        in_specs=placed,
        out_specs=(P("tm", "heads", None), P("tm", "heads", None)),
        check_vma=False,
    )
```

```python
import jax
import jax.numpy as jnp
from jax import lax
from jax.experimental import pallas as pl
from jax.experimental.pallas import tpu as pltpu
from jax.sharding import PartitionSpec as P

HD = 64
MESH = pl.DeviceIdType.MESH
F32 = jnp.float32
BF16 = jnp.bfloat16


def layer_norm(floats, gain):
    centre = jnp.mean(floats, axis=-1, keepdims=True)
    moved = floats - centre
    spread = jnp.mean(moved * moved, axis=-1, keepdims=True)
    return (moved * lax.rsqrt(spread + 1e-06) * gain).astype(BF16)


def dot(a, b):
    return jnp.dot(a, b, preferred_element_type=F32)


def dot_t(a, b):
    return lax.dot_general(a, b, (((1,), (1,)), ((), ())), preferred_element_type=F32)


def iota(shape, axis):
    return lax.broadcasted_iota(jnp.int32, shape, axis)


def attend(queries, keys, values, valid):
    scores = dot_t(queries, keys) * (HD ** -0.5)
    if valid is not None:
        scores = jnp.where(valid, scores, -jnp.inf)
    raised = jnp.exp(scores - jnp.max(scores, axis=-1, keepdims=True))
    total = jnp.sum(raised, axis=-1, keepdims=True)
    return dot(raised.astype(BF16), values) / total


def kernel(
    video, t_gain, t_qkv, t_out, s_gain, s_qkv, s_out, m_gain, m_up, m_down, m_merge,
    block_out, merged,
    vid, w_tqkv, w_out, w_sqkv, w_mlp, w_merge,
    fsend, frecv, frecv_extra, rsend, rsend_extra, rrecv,
    hbuf, sqkv, smix, mix_send, mix_recv, edge_send, edge_recv,
    load_sem, o_sem, oy_sem, w_sem, y_sem, c_sem, f_sem, r_sem, h_sem, x_sem, e_sem,
):
    tm = lax.axis_index("tm")
    hx = lax.axis_index("heads")
    count = lax.axis_size("tm")
    wide = lax.axis_size("heads")
    positions, model = video.shape[0], video.shape[2]
    quarter = positions // wide
    group = count // wide
    width = t_qkv.shape[1]
    heads = width // HD
    home = tm // group
    rank = lax.rem(tm, group)
    last = rank == group - 1
    rows = hbuf.shape[1]
    half = rows // 2

    hidden = m_up.shape[1]
    core = lax.rem(tm, 2)
    ring = lax.rem(tm // 2, 4)

    def peer(step):
        return lax.rem(hx + step, wide)

    def along(step):
        return tm // 8 * 8 + lax.rem(ring + step, 4) * 2 + core

    def remote(source, target, sems, i, **to):
        return pltpu.make_async_remote_copy(
            source, target, sems.at[0, i], sems.at[1, i], device_id=to, device_id_type=MESH
        )

    loads = []
    for i, (source, target) in enumerate(
        (
            (video, vid), (t_qkv, w_tqkv), (m_up, w_mlp.at[0, pl.ds(0, model)]),
            (m_down, w_mlp.at[0, pl.ds(model, hidden)]), (t_out, w_out.at[0, pl.ds(0, width)]),
            (s_out, w_out.at[0, pl.ds(width, width)]), (s_qkv, w_sqkv), (m_merge, w_merge),
        )
    ):
        copy = pltpu.make_async_copy(source, target, load_sem.at[i])
        copy.start()
        loads.append(copy)

    barrier = pltpu.get_barrier_semaphore()

    def other(k):
        side = lax.rem(k, 2)
        return lax.rem(tm + count // 2 + (1 - 2 * side) * ((k + side) // 2) + count, count)

    @pl.loop(0, count - 1)
    def _(k):
        pl.semaphore_signal(barrier, inc=1, device_id={"tm": other(k)}, device_id_type=MESH)

    for step in range(1, wide):
        pl.semaphore_signal(
            barrier, inc=1, device_id={"heads": peer(step)}, device_id_type=MESH
        )

    loads[0].wait()
    loads[1].wait()
    tqkv = w_tqkv[...].reshape(3 * width, model)
    normed = layer_norm(vid[...].reshape(2 * positions, model).astype(F32), t_gain[...])
    fsend[...] = dot_t(normed, tqkv).astype(BF16).reshape(positions, 2, 3 * width)

    pl.semaphore_wait(barrier, count - 1 + wide - 1)

    def first_position(device):
        return (device // group) * quarter + lax.rem(device, group) * 3

    @pl.loop(0, count - 1)
    def _(k):
        to = other(k)
        start = first_position(to)
        pltpu.make_async_remote_copy(
            fsend.at[pl.ds(start, 3)], frecv.at[tm], f_sem.at[0], f_sem.at[1],
            device_id={"tm": to}, device_id_type=MESH,
        ).start()

        @pl.when(lax.rem(to, group) == group - 1)
        def _():
            pltpu.make_async_remote_copy(
                fsend.at[start + 3], frecv_extra.at[tm], f_sem.at[2], f_sem.at[3],
                device_id={"tm": to}, device_id_type=MESH,
            ).start()

    own_start = first_position(tm)
    pltpu.make_async_copy(fsend.at[pl.ds(own_start, 3)], frecv.at[tm], f_sem.at[1]).start()

    @pl.when(last)
    def _():
        pltpu.make_async_copy(fsend.at[own_start + 3], frecv_extra.at[tm], f_sem.at[3]).start()

    others = pl.ds(1, wide - 1)

    def fetch(buffer, rows, sems):
        copies = []
        for step in (2, 1, 3):
            copy = remote(
                buffer.at[0, rows], buffer.at[wide - step, rows], sems, step, heads=peer(step)
            )
            copy.start()
            copies.append(copy)
        return copies

    def send(block, sems, i, to):
        copy = remote(block, block, sems, i, tm=to)
        copy.start()
        return copy

    out_share = w_out.shape[1] // 8
    out_cut = out_share // 32 * 16

    def out_rows(step, part):
        start = (core * 4 + lax.rem(ring + step, 4)) * out_share
        size = (out_cut, out_share - out_cut, out_share)[part]
        return pl.ds(pl.multiple_of(start + (out_cut if part == 1 else 0), 16), size)

    def out_block(step, part):
        return w_out.at[others, out_rows(step, part)]

    mlp_share = w_mlp.shape[1] // 8

    def mlp_rows(step, begin, size):
        quart = lax.rem(ring + tm // 8 + step, 4)
        return pl.ds(pl.multiple_of((core * 4 + quart) * mlp_share + begin, 16), size)

    def mlp_block(step, begin, size):
        return w_mlp.at[others, mlp_rows(step, begin, size)]

    ways = (along(1), along(3), lax.rem(tm + 8, count), lax.rem(tm + count - 8, count))
    sibling = tm + 1 - 2 * core
    for i in (2, 3, 4, 5):
        loads[i].wait()
    out_x = fetch(w_out, out_rows(0, 2), o_sem)
    mlp_x = fetch(w_mlp, mlp_rows(0, 0, mlp_share), w_sem)

    row = iota((rows, 2 * quarter), 0)
    column = iota((rows, 2 * quarter), 1)
    place = lax.rem(row, half)
    order = ((place < quarter) & (column == 2 * place + row // half)).astype(BF16)
    own_video = dot(order, vid[pl.ds(hx * quarter, quarter)].reshape(2 * quarter, model))

    for copy in out_x:
        copy.wait_recv()
    out_y = [
        send(out_block(0, 0), oy_sem, 0, ways[0]),
        send(out_block(0, 1), oy_sem, 1, ways[1]),
        send(out_block(0, 1), oy_sem, 2, ways[0]),
        send(out_block(0, 0), oy_sem, 3, ways[1]),
    ]
    out_y[0].wait_recv()
    out_y.append(send(out_block(3, 0), oy_sem, 4, ways[0]))
    out_y[1].wait_recv()
    out_y.append(send(out_block(1, 1), oy_sem, 5, ways[1]))

    pltpu.make_async_copy(frecv, frecv, f_sem.at[1]).wait()

    def temporal(block):
        parts = []
        for head in range(heads):
            at = head * HD
            parts.append(
                attend(
                    block[:, at : at + HD],
                    block[:, width + at : width + at + HD],
                    block[:, 2 * width + at : 2 * width + at + HD],
                    None,
                )
            )
        mixed = jnp.concatenate(parts, axis=1).astype(BF16)
        return mixed.reshape(count, 2, width)

    for p in range(3):
        rsend[:, p] = temporal(frecv[:, p].reshape(2 * count, 3 * width))

    @pl.when(last)
    def _():
        pltpu.make_async_copy(frecv_extra, frecv_extra, f_sem.at[3]).wait()
        rsend_extra[...] = temporal(frecv_extra[...].reshape(2 * count, 3 * width))

    def send_back(to, local):
        pieces = [(rsend.at[to], rrecv.at[hx, pl.ds(3 * rank, 3)], 0, 1)]
        extra = (rsend_extra.at[to], rrecv.at[hx, 3 * group], 2, 3)

        def go(source, target, send, recv):
            if local:
                pltpu.make_async_copy(source, target, r_sem.at[recv]).start()
            else:
                pltpu.make_async_remote_copy(
                    source, target, r_sem.at[send], r_sem.at[recv],
                    device_id={"tm": to, "heads": home}, device_id_type=MESH,
                ).start()

        go(*pieces[0])

        @pl.when(last)
        def _():
            go(*extra)

    @pl.loop(0, count - 1)
    def _(k):
        send_back(other(k), False)

    @pl.when(home == hx)
    def _():
        send_back(tm, True)

    @pl.when(home != hx)
    def _():
        send_back(tm, False)

    for copy in out_y[2:]:
        copy.wait_recv()
    half_out = w_out.shape[1] // 2
    rows_out = pl.ds(pl.multiple_of(core * half_out, 16), half_out)
    out_given = send(w_out.at[others, rows_out], c_sem, 0, sibling)
    for copy in mlp_x:
        copy.wait_recv()

    pltpu.make_async_copy(
        fsend.at[pl.ds(0, 3 * (count - 1))], fsend.at[pl.ds(0, 3 * (count - 1))], f_sem.at[0]
    ).wait()

    @pl.when(last)
    def _():
        part = fsend.at[pl.ds(0, wide - 1)]
        pltpu.make_async_copy(part, part, f_sem.at[2]).wait()

    @pl.when(jnp.logical_not(last))
    def _():
        part = fsend.at[pl.ds(0, wide)]
        pltpu.make_async_copy(part, part, f_sem.at[2]).wait()

    most = rrecv.at[:, pl.ds(0, 3 * group)]
    pltpu.make_async_copy(most, most, r_sem.at[1]).wait()
    rest = rrecv.at[:, 3 * group]
    pltpu.make_async_copy(rest, rest, r_sem.at[3]).wait()
    part = mlp_share // 2
    mlp_yz = [send(mlp_block(0, i // 2 * part, part), y_sem, i, ways[i]) for i in range(4)]
    given = [send(mlp_block(0, 0, mlp_share), c_sem, 1, sibling)]
    out_given.wait_recv()
    total = own_video
    for slot in range(wide):
        mixed = dot(order, rrecv[peer(slot)].reshape(2 * quarter, width)).astype(BF16)
        total += dot(mixed, w_out[slot, 0:width])
    x1 = total.astype(BF16).astype(F32)

    hbuf[hx] = layer_norm(x1, s_gain[...])
    copies = {}
    for step in (1, 3, 2):
        copies[step] = remote(hbuf.at[hx], hbuf.at[hx], h_sem, step, heads=peer(step))
        copies[step].start()
    loads[6].wait()
    for step in (0, 1, 3, 2):
        if step == 2:
            for copy in mlp_yz:
                copy.wait_recv()
            onward = ((3, 1), (1, 0), (3, 3), (1, 2))
            for i, (whose, place) in enumerate(onward):
                block = mlp_block(whose, place * (part // 2), part // 2)
                mlp_yz.append(send(block, y_sem, 4 + i, ways[i]))
        if step:
            copies[step].wait_recv()
        at = peer(wide - step)
        projected = dot_t(hbuf[at], w_sqkv[...].reshape(3 * width, model))
        for f in range(2):
            sqkv[f, at] = projected[f * half : (f + 1) * half]
    given.append(send(mlp_block(3, 0, mlp_share), c_sem, 2, sibling))
    given.append(send(mlp_block(1, 0, mlp_share), c_sem, 3, sibling))
    keep = lax.rem(iota((1, wide * half), 1), half) < quarter
    for f in range(2):
        block = sqkv[f].reshape(wide * half, 3 * width).astype(BF16)
        for head in range(heads):
            at = head * HD
            smix[:, f, :, at : at + HD] = attend(
                block[:, at : at + HD],
                block[:, width + at : width + at + HD],
                block[:, 2 * width + at : 2 * width + at + HD],
                keep,
            ).reshape(wide, half, HD)
    mix_send[...] = smix[...].reshape(wide, rows, width).astype(BF16)
    mix_copies = []
    for step in (2, 1, 3):
        copy = remote(mix_send.at[peer(step)], mix_recv.at[hx], x_sem, step, heads=peer(step))
        copy.start()
        mix_copies.append(copy)
    for copy in mlp_yz[4:]:
        copy.wait_recv()
    given.append(send(mlp_block(2, 0, mlp_share), c_sem, 4, sibling))
    total = x1 + dot(mix_send[hx], w_out[0, width:])
    for step, copy in zip((2, 1, 3), mix_copies):
        copy.wait_recv()
        total += dot(mix_recv[peer(wide - step)], w_out[wide - step, width:])
    x2 = total.astype(BF16).astype(F32)

    normed = layer_norm(x2, m_gain[...])
    total = x2
    for slot in range(wide):
        if slot == 1:
            for copy in given:
                copy.wait_recv()
        up = dot(normed, w_mlp[slot, 0:model])
        shown = (0.5 * up * (1.0 + lax.erf(up * (0.5 ** 0.5)))).astype(BF16)
        total += dot(shown, w_mlp[slot, model:])
    for f in range(2):
        block_out[:, f] = total[f * half : f * half + quarter].astype(BF16)
    first = total[:half].astype(BF16)
    second = total[half:].astype(BF16)

    edge_send[0:half] = second
    edge_send[half:] = jnp.zeros((edge_send.shape[0] - half, model), BF16)
    to_next = pltpu.make_async_remote_copy(
        edge_send, edge_recv, e_sem.at[0], e_sem.at[1],
        device_id={"tm": lax.rem(tm + 1, count)}, device_id_type=MESH,
    )

    @pl.when(tm < count - 1)
    def _():
        to_next.start()

    loads[7].wait()
    result = dot(first, w_merge[1]) + dot(second, w_merge[2])

    @pl.when(tm > 0)
    def _():
        to_next.wait_recv()

    @pl.when(tm == 0)
    def _():
        edge_recv[...] = jnp.zeros_like(edge_recv)

    result += dot(edge_recv[0:half], w_merge[0])
    merged[0] = result[:quarter].astype(BF16)

    @pl.when(tm < count - 1)
    def _():
        to_next.wait_send()

    @pl.when(home == hx)
    def _():
        part = rsend.at[pl.ds(0, count - 1)]
        pltpu.make_async_copy(part, part, r_sem.at[0]).wait()

        @pl.when(last)
        def _():
            part = rsend_extra.at[pl.ds(0, count - 1)]
            pltpu.make_async_copy(part, part, r_sem.at[2]).wait()

    @pl.when(home != hx)
    def _():
        pltpu.make_async_copy(rsend, rsend, r_sem.at[0]).wait()

        @pl.when(last)
        def _():
            pltpu.make_async_copy(rsend_extra, rsend_extra, r_sem.at[2]).wait()

    for copy in (
        *copies.values(), *mix_copies, *out_x, *out_y, *mlp_x, *mlp_yz, *given, out_given,
    ):
        copy.wait_send()


def local(video, t_gain, t_qkv, t_out, s_gain, s_qkv, s_out, m_gain, m_up, m_down, m_merge):
    count = lax.axis_size("tm")
    wide = lax.axis_size("heads")
    frames, positions, model = video.shape
    width = t_qkv.shape[1]
    hidden = m_up.shape[1]
    quarter = positions // wide
    half = -(-quarter // 8) * 8
    rows = 2 * half
    edge = -(-half // 16) * 16
    vmem = pltpu.VMEM
    dma = pltpu.SemaphoreType.DMA
    in_vmem = pl.BlockSpec(memory_space=pltpu.VMEM)
    anywhere = pl.BlockSpec(memory_space=pl.ANY)
    out, together = pl.pallas_call(
        kernel,
        out_shape=(
            jax.ShapeDtypeStruct((quarter, frames, model), BF16),
            jax.ShapeDtypeStruct((frames // 2, quarter, model), BF16),
        ),
        in_specs=[
            anywhere, in_vmem, anywhere, anywhere, in_vmem, anywhere, anywhere, in_vmem,
            anywhere, anywhere, anywhere,
        ],
        out_specs=(in_vmem, in_vmem),
        scratch_shapes=[
            vmem((positions, frames, model), BF16),
            vmem((3, width, model), BF16),
            vmem((wide, 2 * width, model), BF16),
            vmem((3, width, model), BF16),
            vmem((wide, model + hidden, model), BF16),
            vmem((3, model, model), BF16),
            vmem((positions, 2, 3 * width), BF16),
            vmem((count, 3, 2, 3 * width), BF16),
            vmem((count, 2, 3 * width), BF16),
            vmem((count, 3, 2, width), BF16),
            vmem((count, 2, width), BF16),
            vmem((wide, quarter, 2, width), BF16),
            vmem((wide, rows, model), BF16),
            vmem((2, wide, half, 3 * width), F32),
            vmem((wide, 2, half, width), F32),
            vmem((wide, rows, width), BF16),
            vmem((wide, rows, width), BF16),
            vmem((edge, model), BF16),
            vmem((edge, model), BF16),
            dma((8,)), dma((2, 4)), dma((2, 6)), dma((2, 4)), dma((2, 8)), dma((2, 5)),
            dma((4,)), dma((4,)), dma((2, 4)), dma((2, 4)), dma((2,)),
        ],
        compiler_params=pltpu.CompilerParams(
            collective_id=0, has_side_effects=True, vmem_limit_bytes=60 * 2**20
        ),
    )(
        jnp.swapaxes(video, 0, 1), t_gain, t_qkv, t_out, s_gain, s_qkv, s_out, m_gain,
        m_up, m_down, m_merge,
    )
    return jnp.swapaxes(out, 0, 1), together


def solution(mesh):
    placed = (
        P("tm", None, None),
        P(),
        P(None, "heads", None),
        P("heads", None),
        P(),
        P(None, "heads", None),
        P("heads", None),
        P(),
        P(None, "heads"),
        P("heads", None),
        P(),
    )
    return jax.shard_map(
        local,
        mesh=mesh,
        in_specs=placed,
        out_specs=(P("tm", "heads", None), P("tm", "heads", None)),
        check_vma=False,
    )
```

```python
import jax
import jax.numpy as jnp
from jax import lax
from jax.experimental import pallas as pl
from jax.experimental.pallas import tpu as pltpu
from jax.sharding import PartitionSpec as P

HD = 64
MESH = pl.DeviceIdType.MESH
F32 = jnp.float32
BF16 = jnp.bfloat16


def layer_norm(floats, gain):
    centre = jnp.mean(floats, axis=-1, keepdims=True)
    moved = floats - centre
    spread = jnp.mean(moved * moved, axis=-1, keepdims=True)
    return (moved * lax.rsqrt(spread + 1e-06) * gain).astype(BF16)


def dot(a, b):
    return jnp.dot(a, b, preferred_element_type=F32)


def dot_t(a, b):
    return lax.dot_general(a, b, (((1,), (1,)), ((), ())), preferred_element_type=F32)


def iota(shape, axis):
    return lax.broadcasted_iota(jnp.int32, shape, axis)


def attend(queries, keys, values, valid):
    scores = dot_t(queries, keys) * (HD ** -0.5)
    if valid is not None:
        scores = jnp.where(valid, scores, -jnp.inf)
    raised = jnp.exp(scores - jnp.max(scores, axis=-1, keepdims=True))
    total = jnp.sum(raised, axis=-1, keepdims=True)
    return dot(raised.astype(BF16), values) / total


def kernel(
    video, t_gain, t_qkv, t_out, s_gain, s_qkv, s_out, m_gain, m_up, m_down, m_merge,
    block_out, merged,
    vid, w_tqkv, w_out, w_sqkv, w_mlp, w_merge,
    fsend, frecv, frecv_extra, rsend, rsend_extra, rrecv,
    hbuf, sqkv, smix, mix_send, mix_recv, edge_send, edge_recv,
    load_sem, o_sem, oy_sem, w_sem, y_sem, c_sem, f_sem, r_sem, h_sem, x_sem, e_sem,
):
    tm = lax.axis_index("tm")
    hx = lax.axis_index("heads")
    count = lax.axis_size("tm")
    wide = lax.axis_size("heads")
    positions, model = video.shape[0], video.shape[2]
    quarter = positions // wide
    group = count // wide
    width = t_qkv.shape[1]
    heads = width // HD
    home = tm // group
    rank = lax.rem(tm, group)
    last = rank == group - 1
    rows = hbuf.shape[1]
    half = rows // 2

    hidden = m_up.shape[1]
    core = lax.rem(tm, 2)
    ring = lax.rem(tm // 2, 4)

    def peer(step):
        return lax.rem(hx + step, wide)

    def along(step):
        return tm // 8 * 8 + lax.rem(ring + step, 4) * 2 + core

    def remote(source, target, sems, i, **to):
        return pltpu.make_async_remote_copy(
            source, target, sems.at[0, i], sems.at[1, i], device_id=to, device_id_type=MESH
        )

    loads = []
    for i, (source, target) in enumerate(
        (
            (video, vid), (t_qkv, w_tqkv), (m_up, w_mlp.at[0, pl.ds(0, model)]),
            (m_down, w_mlp.at[0, pl.ds(model, hidden)]), (t_out, w_out.at[0, pl.ds(0, width)]),
            (s_out, w_out.at[0, pl.ds(width, width)]), (s_qkv, w_sqkv), (m_merge, w_merge),
        )
    ):
        copy = pltpu.make_async_copy(source, target, load_sem.at[i])
        copy.start()
        loads.append(copy)

    barrier = pltpu.get_barrier_semaphore()

    def other(k):
        side = lax.rem(k, 2)
        return lax.rem(tm + count // 2 + (1 - 2 * side) * ((k + side) // 2) + count, count)

    @pl.loop(0, count - 1)
    def _(k):
        pl.semaphore_signal(barrier, inc=1, device_id={"tm": other(k)}, device_id_type=MESH)

    for step in range(1, wide):
        pl.semaphore_signal(
            barrier, inc=1, device_id={"heads": peer(step)}, device_id_type=MESH
        )

    loads[0].wait()
    loads[1].wait()
    tqkv = w_tqkv[...].reshape(3 * width, model)
    normed = layer_norm(vid[...].reshape(2 * positions, model).astype(F32), t_gain[...])
    fsend[...] = dot_t(normed, tqkv).astype(BF16).reshape(positions, 2, 3 * width)

    pl.semaphore_wait(barrier, count - 1 + wide - 1)

    def first_position(device):
        return (device // group) * quarter + lax.rem(device, group) * 3

    @pl.loop(0, count - 1)
    def _(k):
        to = other(k)
        start = first_position(to)
        pltpu.make_async_remote_copy(
            fsend.at[pl.ds(start, 3)], frecv.at[tm], f_sem.at[0], f_sem.at[1],
            device_id={"tm": to}, device_id_type=MESH,
        ).start()

        @pl.when(lax.rem(to, group) == group - 1)
        def _():
            pltpu.make_async_remote_copy(
                fsend.at[start + 3], frecv_extra.at[tm], f_sem.at[2], f_sem.at[3],
                device_id={"tm": to}, device_id_type=MESH,
            ).start()

    own_start = first_position(tm)
    pltpu.make_async_copy(fsend.at[pl.ds(own_start, 3)], frecv.at[tm], f_sem.at[1]).start()

    @pl.when(last)
    def _():
        pltpu.make_async_copy(fsend.at[own_start + 3], frecv_extra.at[tm], f_sem.at[3]).start()

    others = pl.ds(1, wide - 1)

    def fetch(buffer, rows, sems, base=0):
        copies = []
        for step in (2, 1, 3):
            copy = remote(
                buffer.at[0, rows], buffer.at[wide - step, rows], sems, base + step,
                heads=peer(step),
            )
            copy.start()
            copies.append(copy)
        return copies

    def send(block, sems, i, to):
        copy = remote(block, block, sems, i, tm=to)
        copy.start()
        return copy

    out_share = w_out.shape[1] // 8
    out_cut = out_share // 32 * 16

    def out_rows(step, part):
        start = (core * 4 + lax.rem(ring + step, 4)) * out_share
        size = (out_cut, out_share - out_cut, out_share)[part]
        return pl.ds(pl.multiple_of(start + (out_cut if part == 1 else 0), 16), size)

    def out_block(step, part):
        return w_out.at[others, out_rows(step, part)]

    mlp_share = w_mlp.shape[1] // 8

    def mlp_rows(step, begin, size):
        quart = lax.rem(ring + tm // 8 + step, 4)
        return pl.ds(pl.multiple_of((core * 4 + quart) * mlp_share + begin, 16), size)

    def mlp_block(step, begin, size):
        return w_mlp.at[others, mlp_rows(step, begin, size)]

    ways = (along(1), along(3), lax.rem(tm + 8, count), lax.rem(tm + count - 8, count))
    sibling = tm + 1 - 2 * core
    for i in (2, 3, 4, 5):
        loads[i].wait()
    out_x = fetch(w_out, out_rows(0, 2), o_sem)
    third = mlp_share // 3
    mlp_x = fetch(w_mlp, mlp_rows(0, 0, third), w_sem)
    mlp_x += fetch(w_mlp, mlp_rows(0, third, 2 * third), w_sem, 4)

    row = iota((rows, 2 * quarter), 0)
    column = iota((rows, 2 * quarter), 1)
    place = lax.rem(row, half)
    order = ((place < quarter) & (column == 2 * place + row // half)).astype(BF16)
    own_video = dot(order, vid[pl.ds(hx * quarter, quarter)].reshape(2 * quarter, model))

    for copy in out_x:
        copy.wait_recv()
    out_y = [
        send(out_block(0, 0), oy_sem, 0, ways[0]),
        send(out_block(0, 1), oy_sem, 1, ways[1]),
        send(out_block(0, 1), oy_sem, 2, ways[0]),
        send(out_block(0, 0), oy_sem, 3, ways[1]),
    ]
    out_y[0].wait_recv()
    out_y.append(send(out_block(3, 0), oy_sem, 4, ways[0]))
    out_y[1].wait_recv()
    out_y.append(send(out_block(1, 1), oy_sem, 5, ways[1]))
    for copy in mlp_x[:3]:
        copy.wait_recv()
    mlp_yz = [send(mlp_block(0, 0, third), y_sem, 8 + i, ways[i]) for i in range(2)]

    pltpu.make_async_copy(frecv, frecv, f_sem.at[1]).wait()

    def temporal(block):
        parts = []
        for head in range(heads):
            at = head * HD
            parts.append(
                attend(
                    block[:, at : at + HD],
                    block[:, width + at : width + at + HD],
                    block[:, 2 * width + at : 2 * width + at + HD],
                    None,
                )
            )
        mixed = jnp.concatenate(parts, axis=1).astype(BF16)
        return mixed.reshape(count, 2, width)

    for p in range(3):
        rsend[:, p] = temporal(frecv[:, p].reshape(2 * count, 3 * width))

    @pl.when(last)
    def _():
        pltpu.make_async_copy(frecv_extra, frecv_extra, f_sem.at[3]).wait()
        rsend_extra[...] = temporal(frecv_extra[...].reshape(2 * count, 3 * width))

    def send_back(to, local):
        pieces = [(rsend.at[to], rrecv.at[hx, pl.ds(3 * rank, 3)], 0, 1)]
        extra = (rsend_extra.at[to], rrecv.at[hx, 3 * group], 2, 3)

        def go(source, target, send, recv):
            if local:
                pltpu.make_async_copy(source, target, r_sem.at[recv]).start()
            else:
                pltpu.make_async_remote_copy(
                    source, target, r_sem.at[send], r_sem.at[recv],
                    device_id={"tm": to, "heads": home}, device_id_type=MESH,
                ).start()

        go(*pieces[0])

        @pl.when(last)
        def _():
            go(*extra)

    @pl.loop(0, count - 1)
    def _(k):
        send_back(other(k), False)

    @pl.when(home == hx)
    def _():
        send_back(tm, True)

    @pl.when(home != hx)
    def _():
        send_back(tm, False)

    for copy in out_y[2:]:
        copy.wait_recv()
    half_out = w_out.shape[1] // 2
    rows_out = pl.ds(pl.multiple_of(core * half_out, 16), half_out)
    out_given = send(w_out.at[others, rows_out], c_sem, 0, sibling)
    for copy in mlp_x[3:]:
        copy.wait_recv()

    pltpu.make_async_copy(
        fsend.at[pl.ds(0, 3 * (count - 1))], fsend.at[pl.ds(0, 3 * (count - 1))], f_sem.at[0]
    ).wait()

    @pl.when(last)
    def _():
        part = fsend.at[pl.ds(0, wide - 1)]
        pltpu.make_async_copy(part, part, f_sem.at[2]).wait()

    @pl.when(jnp.logical_not(last))
    def _():
        part = fsend.at[pl.ds(0, wide)]
        pltpu.make_async_copy(part, part, f_sem.at[2]).wait()

    most = rrecv.at[:, pl.ds(0, 3 * group)]
    pltpu.make_async_copy(most, most, r_sem.at[1]).wait()
    rest = rrecv.at[:, 3 * group]
    pltpu.make_async_copy(rest, rest, r_sem.at[3]).wait()
    mlp_yz += [
        send(mlp_block(0, (1 + i // 2) * third, third), y_sem, i, ways[i]) for i in range(4)
    ]
    part = mlp_share // 4
    given = [send(mlp_block(0, 0, mlp_share), c_sem, 1, sibling)]
    out_given.wait_recv()
    total = own_video
    for slot in range(wide):
        mixed = dot(order, rrecv[peer(slot)].reshape(2 * quarter, width)).astype(BF16)
        total += dot(mixed, w_out[slot, 0:width])
    x1 = total.astype(BF16).astype(F32)

    hbuf[hx] = layer_norm(x1, s_gain[...])
    upper, lower = pl.ds(0, rows // 32 * 16), pl.ds(rows // 32 * 16, rows - rows // 32 * 16)

    def pass_on(whose, part, i, step):
        block = hbuf.at[whose, part]
        copy = remote(block, block, h_sem, i, heads=peer(step))
        copy.start()
        return copy

    copies = [
        pass_on(hx, upper, 0, 1),
        pass_on(hx, lower, 1, 3),
        pass_on(hx, lower, 2, 1),
        pass_on(hx, upper, 3, 3),
    ]
    loads[6].wait()
    for step in (0, 1, 3, 2):
        if step == 2:
            for copy in mlp_yz:
                copy.wait_recv()
            onward = ((3, 1), (1, 0), (3, 3), (1, 2))
            for i, (whose, place) in enumerate(onward):
                block = mlp_block(whose, place * part, part)
                mlp_yz.append(send(block, y_sem, 4 + i, ways[i]))
            given.append(send(mlp_block(3, 0, mlp_share), c_sem, 2, sibling))
            given.append(send(mlp_block(1, 0, mlp_share), c_sem, 3, sibling))
        if step == 1:
            copies[0].wait_recv()
            copies.append(pass_on(peer(3), upper, 4, 1))
            copies[1].wait_recv()
            copies.append(pass_on(peer(1), lower, 5, 3))
        for i in ((), (2,), (4, 5), (3,))[step]:
            copies[i].wait_recv()
        at = peer(wide - step)
        projected = dot_t(hbuf[at], w_sqkv[...].reshape(3 * width, model))
        for f in range(2):
            sqkv[f, at] = projected[f * half : (f + 1) * half]
    keep = lax.rem(iota((1, wide * half), 1), half) < quarter
    for f in range(2):
        block = sqkv[f].reshape(wide * half, 3 * width).astype(BF16)
        for head in range(heads):
            at = head * HD
            smix[:, f, :, at : at + HD] = attend(
                block[:, at : at + HD],
                block[:, width + at : width + at + HD],
                block[:, 2 * width + at : 2 * width + at + HD],
                keep,
            ).reshape(wide, half, HD)
    mix_send[...] = smix[...].reshape(wide, rows, width).astype(BF16)
    mix_copies = []
    for step in (2, 1, 3):
        copy = remote(mix_send.at[peer(step)], mix_recv.at[hx], x_sem, step, heads=peer(step))
        copy.start()
        mix_copies.append(copy)
    for copy in mlp_yz[6:]:
        copy.wait_recv()
    given.append(send(mlp_block(2, 0, mlp_share), c_sem, 4, sibling))
    total = x1 + dot(mix_send[hx], w_out[0, width:])
    for step, copy in zip((2, 1, 3), mix_copies):
        copy.wait_recv()
        total += dot(mix_recv[peer(wide - step)], w_out[wide - step, width:])
    x2 = total.astype(BF16).astype(F32)

    normed = layer_norm(x2, m_gain[...])
    total = x2
    for slot in range(wide):
        if slot == 1:
            for copy in given:
                copy.wait_recv()
        up = dot(normed, w_mlp[slot, 0:model])
        shown = (0.5 * up * (1.0 + lax.erf(up * (0.5 ** 0.5)))).astype(BF16)
        total += dot(shown, w_mlp[slot, model:])
    for f in range(2):
        block_out[:, f] = total[f * half : f * half + quarter].astype(BF16)
    first = total[:half].astype(BF16)
    second = total[half:].astype(BF16)

    edge_send[0:half] = second
    edge_send[half:] = jnp.zeros((edge_send.shape[0] - half, model), BF16)
    to_next = pltpu.make_async_remote_copy(
        edge_send, edge_recv, e_sem.at[0], e_sem.at[1],
        device_id={"tm": lax.rem(tm + 1, count)}, device_id_type=MESH,
    )

    @pl.when(tm < count - 1)
    def _():
        to_next.start()

    loads[7].wait()
    result = dot(first, w_merge[1]) + dot(second, w_merge[2])

    @pl.when(tm > 0)
    def _():
        to_next.wait_recv()

    @pl.when(tm == 0)
    def _():
        edge_recv[...] = jnp.zeros_like(edge_recv)

    result += dot(edge_recv[0:half], w_merge[0])
    merged[0] = result[:quarter].astype(BF16)

    @pl.when(tm < count - 1)
    def _():
        to_next.wait_send()

    @pl.when(home == hx)
    def _():
        part = rsend.at[pl.ds(0, count - 1)]
        pltpu.make_async_copy(part, part, r_sem.at[0]).wait()

        @pl.when(last)
        def _():
            part = rsend_extra.at[pl.ds(0, count - 1)]
            pltpu.make_async_copy(part, part, r_sem.at[2]).wait()

    @pl.when(home != hx)
    def _():
        pltpu.make_async_copy(rsend, rsend, r_sem.at[0]).wait()

        @pl.when(last)
        def _():
            pltpu.make_async_copy(rsend_extra, rsend_extra, r_sem.at[2]).wait()

    for copy in (
        *copies, *mix_copies, *out_x, *out_y, *mlp_x, *mlp_yz, *given, out_given,
    ):
        copy.wait_send()


def local(video, t_gain, t_qkv, t_out, s_gain, s_qkv, s_out, m_gain, m_up, m_down, m_merge):
    count = lax.axis_size("tm")
    wide = lax.axis_size("heads")
    frames, positions, model = video.shape
    width = t_qkv.shape[1]
    hidden = m_up.shape[1]
    quarter = positions // wide
    half = -(-quarter // 8) * 8
    rows = 2 * half
    edge = -(-half // 16) * 16
    vmem = pltpu.VMEM
    dma = pltpu.SemaphoreType.DMA
    in_vmem = pl.BlockSpec(memory_space=pltpu.VMEM)
    anywhere = pl.BlockSpec(memory_space=pl.ANY)
    out, together = pl.pallas_call(
        kernel,
        out_shape=(
            jax.ShapeDtypeStruct((quarter, frames, model), BF16),
            jax.ShapeDtypeStruct((frames // 2, quarter, model), BF16),
        ),
        in_specs=[
            anywhere, in_vmem, anywhere, anywhere, in_vmem, anywhere, anywhere, in_vmem,
            anywhere, anywhere, anywhere,
        ],
        out_specs=(in_vmem, in_vmem),
        scratch_shapes=[
            vmem((positions, frames, model), BF16),
            vmem((3, width, model), BF16),
            vmem((wide, 2 * width, model), BF16),
            vmem((3, width, model), BF16),
            vmem((wide, model + hidden, model), BF16),
            vmem((3, model, model), BF16),
            vmem((positions, 2, 3 * width), BF16),
            vmem((count, 3, 2, 3 * width), BF16),
            vmem((count, 2, 3 * width), BF16),
            vmem((count, 3, 2, width), BF16),
            vmem((count, 2, width), BF16),
            vmem((wide, quarter, 2, width), BF16),
            vmem((wide, rows, model), BF16),
            vmem((2, wide, half, 3 * width), F32),
            vmem((wide, 2, half, width), F32),
            vmem((wide, rows, width), BF16),
            vmem((wide, rows, width), BF16),
            vmem((edge, model), BF16),
            vmem((edge, model), BF16),
            dma((8,)), dma((2, 4)), dma((2, 6)), dma((2, 8)), dma((2, 10)), dma((2, 5)),
            dma((4,)), dma((4,)), dma((2, 6)), dma((2, 4)), dma((2,)),
        ],
        compiler_params=pltpu.CompilerParams(
            collective_id=0, has_side_effects=True, vmem_limit_bytes=107 * 2**19
        ),
    )(
        jnp.swapaxes(video, 0, 1), t_gain, t_qkv, t_out, s_gain, s_qkv, s_out, m_gain,
        m_up, m_down, m_merge,
    )
    return jnp.swapaxes(out, 0, 1), together


def solution(mesh):
    placed = (
        P("tm", None, None),
        P(),
        P(None, "heads", None),
        P("heads", None),
        P(),
        P(None, "heads", None),
        P("heads", None),
        P(),
        P(None, "heads"),
        P("heads", None),
        P(),
    )
    return jax.shard_map(
        local,
        mesh=mesh,
        in_specs=placed,
        out_specs=(P("tm", "heads", None), P("tm", "heads", None)),
        check_vma=False,
    )
```

```python
import jax
import jax.numpy as jnp
from jax import lax
from jax.experimental import pallas as pl
from jax.experimental.pallas import tpu as pltpu
from jax.sharding import PartitionSpec as P

HD = 64
MESH = pl.DeviceIdType.MESH
F32 = jnp.float32
BF16 = jnp.bfloat16


def layer_norm(floats, gain):
    centre = jnp.mean(floats, axis=-1, keepdims=True)
    moved = floats - centre
    spread = jnp.mean(moved * moved, axis=-1, keepdims=True)
    return (moved * lax.rsqrt(spread + 1e-06) * gain).astype(BF16)


def dot(a, b):
    return jnp.dot(a, b, preferred_element_type=F32)


def dot_t(a, b):
    return lax.dot_general(a, b, (((1,), (1,)), ((), ())), preferred_element_type=F32)


def iota(shape, axis):
    return lax.broadcasted_iota(jnp.int32, shape, axis)


def attend(queries, keys, values, valid):
    scores = dot_t(queries, keys) * (HD ** -0.5)
    if valid is not None:
        scores = jnp.where(valid, scores, -jnp.inf)
    raised = jnp.exp(scores - jnp.max(scores, axis=-1, keepdims=True))
    total = jnp.sum(raised, axis=-1, keepdims=True)
    return dot(raised.astype(BF16), values) / total


def kernel(
    video, t_gain, t_qkv, t_out, s_gain, s_qkv, s_out, m_gain, m_up, m_down, m_merge,
    block_out, merged,
    vid, w_tqkv, w_out, w_sqkv, w_mlp, w_merge,
    fsend, frecv, frecv_extra, rsend, rsend_extra, rrecv,
    hbuf, sqkv, smix, mix_send, mix_recv, edge_send, edge_recv,
    load_sem, o_sem, oy_sem, w_sem, y_sem, c_sem, f_sem, r_sem, h_sem, x_sem, e_sem,
):
    tm = lax.axis_index("tm")
    hx = lax.axis_index("heads")
    count = lax.axis_size("tm")
    wide = lax.axis_size("heads")
    positions, model = video.shape[0], video.shape[2]
    quarter = positions // wide
    group = count // wide
    width = t_qkv.shape[1]
    heads = width // HD
    home = tm // group
    rank = lax.rem(tm, group)
    last = rank == group - 1
    rows = hbuf.shape[1]
    half = rows // 2

    hidden = m_up.shape[1]
    core = lax.rem(tm, 2)
    ring = lax.rem(tm // 2, 4)

    def peer(step):
        return lax.rem(hx + step, wide)

    def along(step):
        return tm // 8 * 8 + lax.rem(ring + step, 4) * 2 + core

    def remote(source, target, sems, i, **to):
        return pltpu.make_async_remote_copy(
            source, target, sems.at[0, i], sems.at[1, i], device_id=to, device_id_type=MESH
        )

    loads = []
    for i, (source, target) in enumerate(
        (
            (video, vid), (t_qkv, w_tqkv), (m_up, w_mlp.at[0, pl.ds(0, model)]),
            (m_down, w_mlp.at[0, pl.ds(model, hidden)]), (t_out, w_out.at[0, pl.ds(0, width)]),
            (s_out, w_out.at[0, pl.ds(width, width)]), (s_qkv, w_sqkv), (m_merge, w_merge),
        )
    ):
        copy = pltpu.make_async_copy(source, target, load_sem.at[i])
        copy.start()
        loads.append(copy)

    barrier = pltpu.get_barrier_semaphore()

    def other(k):
        side = lax.rem(k, 2)
        return lax.rem(tm + count // 2 + (1 - 2 * side) * ((k + side) // 2) + count, count)

    @pl.loop(0, count - 1)
    def _(k):
        pl.semaphore_signal(barrier, inc=1, device_id={"tm": other(k)}, device_id_type=MESH)

    for step in range(1, wide):
        pl.semaphore_signal(
            barrier, inc=1, device_id={"heads": peer(step)}, device_id_type=MESH
        )

    loads[0].wait()
    loads[1].wait()
    tqkv = w_tqkv[...].reshape(3 * width, model)
    normed = layer_norm(vid[...].reshape(2 * positions, model).astype(F32), t_gain[...])
    fsend[...] = dot_t(normed, tqkv).astype(BF16).reshape(positions, 2, 3 * width)

    pl.semaphore_wait(barrier, count - 1 + wide - 1)

    def first_position(device):
        return (device // group) * quarter + lax.rem(device, group) * 3

    others = pl.ds(1, wide - 1)

    def fetch(buffer, rows, sems, base=0):
        copies = []
        for step in (2, 1, 3):
            copy = remote(
                buffer.at[0, rows], buffer.at[wide - step, rows], sems, base + step,
                heads=peer(step),
            )
            copy.start()
            copies.append(copy)
        return copies

    def send(block, sems, i, to):
        copy = remote(block, block, sems, i, tm=to)
        copy.start()
        return copy

    out_share = w_out.shape[1] // 8
    out_cut = out_share // 32 * 16

    def out_rows(step, part):
        start = (core * 4 + lax.rem(ring + step, 4)) * out_share
        size = (out_cut, out_share - out_cut, out_share)[part]
        return pl.ds(pl.multiple_of(start + (out_cut if part == 1 else 0), 16), size)

    def out_block(step, part):
        return w_out.at[others, out_rows(step, part)]

    mlp_share = w_mlp.shape[1] // 8

    def mlp_rows(step, begin, size):
        quart = lax.rem(ring + tm // 8 + step, 4)
        return pl.ds(pl.multiple_of((core * 4 + quart) * mlp_share + begin, 16), size)

    def mlp_block(step, begin, size):
        return w_mlp.at[others, mlp_rows(step, begin, size)]

    ways = (along(1), along(3), lax.rem(tm + 8, count), lax.rem(tm + count - 8, count))
    sibling = tm + 1 - 2 * core
    for i in (2, 3, 4, 5):
        loads[i].wait()
    out_x = fetch(w_out, out_rows(0, 2), o_sem)
    third = mlp_share // 3
    mlp_x = fetch(w_mlp, mlp_rows(0, 0, third), w_sem)
    mlp_x += fetch(w_mlp, mlp_rows(0, third, 2 * third), w_sem, 4)

    @pl.loop(0, count - 1)
    def _(k):
        to = other(k)
        start = first_position(to)
        pltpu.make_async_remote_copy(
            fsend.at[pl.ds(start, 3)], frecv.at[tm], f_sem.at[0], f_sem.at[1],
            device_id={"tm": to}, device_id_type=MESH,
        ).start()

        @pl.when(lax.rem(to, group) == group - 1)
        def _():
            pltpu.make_async_remote_copy(
                fsend.at[start + 3], frecv_extra.at[tm], f_sem.at[2], f_sem.at[3],
                device_id={"tm": to}, device_id_type=MESH,
            ).start()

    own_start = first_position(tm)
    pltpu.make_async_copy(fsend.at[pl.ds(own_start, 3)], frecv.at[tm], f_sem.at[1]).start()

    @pl.when(last)
    def _():
        pltpu.make_async_copy(fsend.at[own_start + 3], frecv_extra.at[tm], f_sem.at[3]).start()

    row = iota((rows, 2 * quarter), 0)
    column = iota((rows, 2 * quarter), 1)
    place = lax.rem(row, half)
    order = ((place < quarter) & (column == 2 * place + row // half)).astype(BF16)
    own_video = dot(order, vid[pl.ds(hx * quarter, quarter)].reshape(2 * quarter, model))

    for copy in out_x:
        copy.wait_recv()
    out_y = [
        send(out_block(0, 0), oy_sem, 0, ways[0]),
        send(out_block(0, 1), oy_sem, 1, ways[1]),
        send(out_block(0, 1), oy_sem, 2, ways[0]),
        send(out_block(0, 0), oy_sem, 3, ways[1]),
    ]
    out_y[0].wait_recv()
    out_y.append(send(out_block(3, 0), oy_sem, 4, ways[0]))
    out_y[1].wait_recv()
    out_y.append(send(out_block(1, 1), oy_sem, 5, ways[1]))
    for copy in mlp_x[:3]:
        copy.wait_recv()
    mlp_yz = [send(mlp_block(0, 0, third), y_sem, 8 + i, ways[i]) for i in range(2)]

    pltpu.make_async_copy(frecv, frecv, f_sem.at[1]).wait()

    def temporal(block):
        parts = []
        for head in range(heads):
            at = head * HD
            parts.append(
                attend(
                    block[:, at : at + HD],
                    block[:, width + at : width + at + HD],
                    block[:, 2 * width + at : 2 * width + at + HD],
                    None,
                )
            )
        mixed = jnp.concatenate(parts, axis=1).astype(BF16)
        return mixed.reshape(count, 2, width)

    for p in range(3):
        rsend[:, p] = temporal(frecv[:, p].reshape(2 * count, 3 * width))

    @pl.when(last)
    def _():
        pltpu.make_async_copy(frecv_extra, frecv_extra, f_sem.at[3]).wait()
        rsend_extra[...] = temporal(frecv_extra[...].reshape(2 * count, 3 * width))

    def send_back(to, local):
        pieces = [(rsend.at[to], rrecv.at[hx, pl.ds(3 * rank, 3)], 0, 1)]
        extra = (rsend_extra.at[to], rrecv.at[hx, 3 * group], 2, 3)

        def go(source, target, send, recv):
            if local:
                pltpu.make_async_copy(source, target, r_sem.at[recv]).start()
            else:
                pltpu.make_async_remote_copy(
                    source, target, r_sem.at[send], r_sem.at[recv],
                    device_id={"tm": to, "heads": home}, device_id_type=MESH,
                ).start()

        go(*pieces[0])

        @pl.when(last)
        def _():
            go(*extra)

    @pl.loop(0, count - 1)
    def _(k):
        send_back(other(k), False)

    @pl.when(home == hx)
    def _():
        send_back(tm, True)

    @pl.when(home != hx)
    def _():
        send_back(tm, False)

    for copy in out_y[2:]:
        copy.wait_recv()
    half_out = w_out.shape[1] // 2
    rows_out = pl.ds(pl.multiple_of(core * half_out, 16), half_out)
    out_given = send(w_out.at[others, rows_out], c_sem, 0, sibling)
    for copy in mlp_x[3:]:
        copy.wait_recv()

    pltpu.make_async_copy(
        fsend.at[pl.ds(0, 3 * (count - 1))], fsend.at[pl.ds(0, 3 * (count - 1))], f_sem.at[0]
    ).wait()

    @pl.when(last)
    def _():
        part = fsend.at[pl.ds(0, wide - 1)]
        pltpu.make_async_copy(part, part, f_sem.at[2]).wait()

    @pl.when(jnp.logical_not(last))
    def _():
        part = fsend.at[pl.ds(0, wide)]
        pltpu.make_async_copy(part, part, f_sem.at[2]).wait()

    most = rrecv.at[:, pl.ds(0, 3 * group)]
    pltpu.make_async_copy(most, most, r_sem.at[1]).wait()
    rest = rrecv.at[:, 3 * group]
    pltpu.make_async_copy(rest, rest, r_sem.at[3]).wait()
    mlp_yz += [
        send(mlp_block(0, (1 + i // 2) * third, third), y_sem, i, ways[i]) for i in range(4)
    ]
    part = mlp_share // 4
    given = [send(mlp_block(0, 0, mlp_share), c_sem, 1, sibling)]
    out_given.wait_recv()
    total = own_video
    for slot in range(wide):
        mixed = dot(order, rrecv[peer(slot)].reshape(2 * quarter, width)).astype(BF16)
        total += dot(mixed, w_out[slot, 0:width])
    x1 = total.astype(BF16).astype(F32)

    hbuf[hx] = layer_norm(x1, s_gain[...])
    upper, lower = pl.ds(0, rows // 32 * 16), pl.ds(rows // 32 * 16, rows - rows // 32 * 16)

    def pass_on(whose, part, i, step):
        block = hbuf.at[whose, part]
        copy = remote(block, block, h_sem, i, heads=peer(step))
        copy.start()
        return copy

    copies = [
        pass_on(hx, upper, 0, 1),
        pass_on(hx, lower, 1, 3),
        pass_on(hx, lower, 2, 1),
        pass_on(hx, upper, 3, 3),
    ]
    loads[6].wait()
    for step in (0, 1, 3, 2):
        if step == 2:
            for copy in mlp_yz:
                copy.wait_recv()
            onward = ((3, 1), (1, 0), (3, 3), (1, 2))
            for i, (whose, place) in enumerate(onward):
                block = mlp_block(whose, place * part, part)
                mlp_yz.append(send(block, y_sem, 4 + i, ways[i]))
            given.append(send(mlp_block(3, 0, mlp_share), c_sem, 2, sibling))
            given.append(send(mlp_block(1, 0, mlp_share), c_sem, 3, sibling))
        if step == 1:
            copies[0].wait_recv()
            copies.append(pass_on(peer(3), upper, 4, 1))
            copies[1].wait_recv()
            copies.append(pass_on(peer(1), lower, 5, 3))
        for i in ((), (2,), (4, 5), (3,))[step]:
            copies[i].wait_recv()
        at = peer(wide - step)
        projected = dot_t(hbuf[at], w_sqkv[...].reshape(3 * width, model))
        for f in range(2):
            sqkv[f, at] = projected[f * half : (f + 1) * half]
    keep = lax.rem(iota((1, wide * half), 1), half) < quarter
    for f in range(2):
        block = sqkv[f].reshape(wide * half, 3 * width).astype(BF16)
        for head in range(heads):
            at = head * HD
            smix[:, f, :, at : at + HD] = attend(
                block[:, at : at + HD],
                block[:, width + at : width + at + HD],
                block[:, 2 * width + at : 2 * width + at + HD],
                keep,
            ).reshape(wide, half, HD)
    mix_send[...] = smix[...].reshape(wide, rows, width).astype(BF16)
    mix_copies = []
    for step in (2, 1, 3):
        copy = remote(mix_send.at[peer(step)], mix_recv.at[hx], x_sem, step, heads=peer(step))
        copy.start()
        mix_copies.append(copy)
    for copy in mlp_yz[6:]:
        copy.wait_recv()
    given.append(send(mlp_block(2, 0, mlp_share), c_sem, 4, sibling))
    total = x1 + dot(mix_send[hx], w_out[0, width:])
    for step, copy in zip((2, 1, 3), mix_copies):
        copy.wait_recv()
        total += dot(mix_recv[peer(wide - step)], w_out[wide - step, width:])
    x2 = total.astype(BF16).astype(F32)

    normed = layer_norm(x2, m_gain[...])
    total = x2
    for slot in range(wide):
        if slot == 1:
            for copy in given:
                copy.wait_recv()
        up = dot(normed, w_mlp[slot, 0:model])
        shown = (0.5 * up * (1.0 + lax.erf(up * (0.5 ** 0.5)))).astype(BF16)
        total += dot(shown, w_mlp[slot, model:])
    for f in range(2):
        block_out[:, f] = total[f * half : f * half + quarter].astype(BF16)
    first = total[:half].astype(BF16)
    second = total[half:].astype(BF16)

    edge_send[0:half] = second
    edge_send[half:] = jnp.zeros((edge_send.shape[0] - half, model), BF16)
    to_next = pltpu.make_async_remote_copy(
        edge_send, edge_recv, e_sem.at[0], e_sem.at[1],
        device_id={"tm": lax.rem(tm + 1, count)}, device_id_type=MESH,
    )

    @pl.when(tm < count - 1)
    def _():
        to_next.start()

    loads[7].wait()
    result = dot(first, w_merge[1]) + dot(second, w_merge[2])

    @pl.when(tm > 0)
    def _():
        to_next.wait_recv()

    @pl.when(tm == 0)
    def _():
        edge_recv[...] = jnp.zeros_like(edge_recv)

    result += dot(edge_recv[0:half], w_merge[0])
    merged[0] = result[:quarter].astype(BF16)

    @pl.when(tm < count - 1)
    def _():
        to_next.wait_send()

    @pl.when(home == hx)
    def _():
        part = rsend.at[pl.ds(0, count - 1)]
        pltpu.make_async_copy(part, part, r_sem.at[0]).wait()

        @pl.when(last)
        def _():
            part = rsend_extra.at[pl.ds(0, count - 1)]
            pltpu.make_async_copy(part, part, r_sem.at[2]).wait()

    @pl.when(home != hx)
    def _():
        pltpu.make_async_copy(rsend, rsend, r_sem.at[0]).wait()

        @pl.when(last)
        def _():
            pltpu.make_async_copy(rsend_extra, rsend_extra, r_sem.at[2]).wait()

    for copy in (
        *copies, *mix_copies, *out_x, *out_y, *mlp_x, *mlp_yz, *given, out_given,
    ):
        copy.wait_send()


def local(video, t_gain, t_qkv, t_out, s_gain, s_qkv, s_out, m_gain, m_up, m_down, m_merge):
    count = lax.axis_size("tm")
    wide = lax.axis_size("heads")
    frames, positions, model = video.shape
    width = t_qkv.shape[1]
    hidden = m_up.shape[1]
    quarter = positions // wide
    half = -(-quarter // 8) * 8
    rows = 2 * half
    edge = -(-half // 16) * 16
    vmem = pltpu.VMEM
    dma = pltpu.SemaphoreType.DMA
    in_vmem = pl.BlockSpec(memory_space=pltpu.VMEM)
    anywhere = pl.BlockSpec(memory_space=pl.ANY)
    out, together = pl.pallas_call(
        kernel,
        out_shape=(
            jax.ShapeDtypeStruct((quarter, frames, model), BF16),
            jax.ShapeDtypeStruct((frames // 2, quarter, model), BF16),
        ),
        in_specs=[
            anywhere, in_vmem, anywhere, anywhere, in_vmem, anywhere, anywhere, in_vmem,
            anywhere, anywhere, anywhere,
        ],
        out_specs=(in_vmem, in_vmem),
        scratch_shapes=[
            vmem((positions, frames, model), BF16),
            vmem((3, width, model), BF16),
            vmem((wide, 2 * width, model), BF16),
            vmem((3, width, model), BF16),
            vmem((wide, model + hidden, model), BF16),
            vmem((3, model, model), BF16),
            vmem((positions, 2, 3 * width), BF16),
            vmem((count, 3, 2, 3 * width), BF16),
            vmem((count, 2, 3 * width), BF16),
            vmem((count, 3, 2, width), BF16),
            vmem((count, 2, width), BF16),
            vmem((wide, quarter, 2, width), BF16),
            vmem((wide, rows, model), BF16),
            vmem((2, wide, half, 3 * width), F32),
            vmem((wide, 2, half, width), F32),
            vmem((wide, rows, width), BF16),
            vmem((wide, rows, width), BF16),
            vmem((edge, model), BF16),
            vmem((edge, model), BF16),
            dma((8,)), dma((2, 4)), dma((2, 6)), dma((2, 8)), dma((2, 10)), dma((2, 5)),
            dma((4,)), dma((4,)), dma((2, 6)), dma((2, 4)), dma((2,)),
        ],
        compiler_params=pltpu.CompilerParams(
            collective_id=0, has_side_effects=True, vmem_limit_bytes=107 * 2**19
        ),
    )(
        jnp.swapaxes(video, 0, 1), t_gain, t_qkv, t_out, s_gain, s_qkv, s_out, m_gain,
        m_up, m_down, m_merge,
    )
    return jnp.swapaxes(out, 0, 1), together


def solution(mesh):
    placed = (
        P("tm", None, None),
        P(),
        P(None, "heads", None),
        P("heads", None),
        P(),
        P(None, "heads", None),
        P("heads", None),
        P(),
        P(None, "heads"),
        P("heads", None),
        P(),
    )
    return jax.shard_map(
        local,
        mesh=mesh,
        in_specs=placed,
        out_specs=(P("tm", "heads", None), P("tm", "heads", None)),
        check_vma=False,
    )
```

```python
import jax
import jax.numpy as jnp
from jax import lax
from jax.experimental import pallas as pl
from jax.experimental.pallas import tpu as pltpu
from jax.sharding import PartitionSpec as P

HD = 64
MESH = pl.DeviceIdType.MESH
F32 = jnp.float32
BF16 = jnp.bfloat16


def layer_norm(floats, gain):
    centre = jnp.mean(floats, axis=-1, keepdims=True)
    moved = floats - centre
    spread = jnp.mean(moved * moved, axis=-1, keepdims=True)
    return (moved * lax.rsqrt(spread + 1e-06) * gain).astype(BF16)


def dot(a, b):
    return jnp.dot(a, b, preferred_element_type=F32)


def dot_t(a, b):
    return lax.dot_general(a, b, (((1,), (1,)), ((), ())), preferred_element_type=F32)


def iota(shape, axis):
    return lax.broadcasted_iota(jnp.int32, shape, axis)


def attend(queries, keys, values, valid):
    scores = dot_t(queries * BF16(HD ** -0.5), keys)
    if valid is not None:
        scores = jnp.where(valid, scores, -jnp.inf)
    raised = jnp.exp(scores - jnp.max(scores, axis=-1, keepdims=True))
    total = jnp.sum(raised, axis=-1, keepdims=True)
    return dot(raised.astype(BF16), values) / total


def kernel(
    video, t_gain, t_qkv, t_out, s_gain, s_qkv, s_out, m_gain, m_up, m_down, m_merge,
    block_out, merged,
    vid, w_tqkv, w_out, w_sqkv, w_mlp, w_merge,
    fsend, frecv, frecv_extra, rsend, rsend_extra, rrecv,
    hbuf, sqkv, smix, mix_send, mix_recv, edge_send, edge_recv,
    load_sem, o_sem, oy_sem, w_sem, y_sem, c_sem, f_sem, r_sem, h_sem, x_sem, e_sem,
):
    tm = lax.axis_index("tm")
    hx = lax.axis_index("heads")
    count = lax.axis_size("tm")
    wide = lax.axis_size("heads")
    positions, model = video.shape[0], video.shape[2]
    quarter = positions // wide
    group = count // wide
    width = t_qkv.shape[1]
    heads = width // HD
    home = tm // group
    rank = lax.rem(tm, group)
    last = rank == group - 1
    rows = hbuf.shape[1]
    half = rows // 2

    hidden = m_up.shape[1]
    core = lax.rem(tm, 2)
    ring = lax.rem(tm // 2, 4)

    def peer(step):
        return lax.rem(hx + step, wide)

    def along(step):
        return tm // 8 * 8 + lax.rem(ring + step, 4) * 2 + core

    def remote(source, target, sems, i, **to):
        return pltpu.make_async_remote_copy(
            source, target, sems.at[0, i], sems.at[1, i], device_id=to, device_id_type=MESH
        )

    loads = []
    for i, (source, target) in enumerate(
        (
            (video, vid), (t_qkv, w_tqkv), (m_up, w_mlp.at[0, pl.ds(0, model)]),
            (m_down, w_mlp.at[0, pl.ds(model, hidden)]), (t_out, w_out.at[0, pl.ds(0, width)]),
            (s_out, w_out.at[0, pl.ds(width, width)]), (s_qkv, w_sqkv), (m_merge, w_merge),
        )
    ):
        copy = pltpu.make_async_copy(source, target, load_sem.at[i])
        copy.start()
        loads.append(copy)

    barrier = pltpu.get_barrier_semaphore()

    def other(k):
        side = lax.rem(k, 2)
        return lax.rem(tm + count // 2 + (1 - 2 * side) * ((k + side) // 2) + count, count)

    @pl.loop(0, count - 1)
    def _(k):
        pl.semaphore_signal(barrier, inc=1, device_id={"tm": other(k)}, device_id_type=MESH)

    for step in range(1, wide):
        pl.semaphore_signal(
            barrier, inc=1, device_id={"heads": peer(step)}, device_id_type=MESH
        )

    loads[0].wait()
    loads[1].wait()
    tqkv = w_tqkv[...].reshape(3 * width, model)
    normed = layer_norm(vid[...].reshape(2 * positions, model).astype(F32), t_gain[...])
    fsend[...] = dot_t(normed, tqkv).astype(BF16).reshape(positions, 2, 3 * width)

    pl.semaphore_wait(barrier, count - 1 + wide - 1)

    def first_position(device):
        return (device // group) * quarter + lax.rem(device, group) * 3

    others = pl.ds(1, wide - 1)

    def fetch(buffer, rows, sems, base=0):
        copies = []
        for step in (2, 1, 3):
            copy = remote(
                buffer.at[0, rows], buffer.at[wide - step, rows], sems, base + step,
                heads=peer(step),
            )
            copy.start()
            copies.append(copy)
        return copies

    def send(block, sems, i, to):
        copy = remote(block, block, sems, i, tm=to)
        copy.start()
        return copy

    out_share = w_out.shape[1] // 8
    out_cut = out_share // 32 * 16

    def out_rows(step, part):
        start = (core * 4 + lax.rem(ring + step, 4)) * out_share
        size = (out_cut, out_share - out_cut, out_share)[part]
        return pl.ds(pl.multiple_of(start + (out_cut if part == 1 else 0), 16), size)

    def out_block(step, part):
        return w_out.at[others, out_rows(step, part)]

    mlp_share = w_mlp.shape[1] // 8

    def mlp_rows(step, begin, size):
        quart = lax.rem(ring + tm // 8 + step, 4)
        return pl.ds(pl.multiple_of((core * 4 + quart) * mlp_share + begin, 16), size)

    def mlp_block(step, begin, size):
        return w_mlp.at[others, mlp_rows(step, begin, size)]

    ways = (along(1), along(3), lax.rem(tm + 8, count), lax.rem(tm + count - 8, count))
    sibling = tm + 1 - 2 * core
    for i in (2, 3, 4, 5):
        loads[i].wait()
    out_x = fetch(w_out, out_rows(0, 2), o_sem)
    third = mlp_share // 3
    mlp_x = fetch(w_mlp, mlp_rows(0, 0, third), w_sem)
    mlp_x += fetch(w_mlp, mlp_rows(0, third, 2 * third), w_sem, 4)

    @pl.loop(0, count - 1)
    def _(k):
        to = other(k)
        start = first_position(to)
        pltpu.make_async_remote_copy(
            fsend.at[pl.ds(start, 3)], frecv.at[tm], f_sem.at[0], f_sem.at[1],
            device_id={"tm": to}, device_id_type=MESH,
        ).start()

        @pl.when(lax.rem(to, group) == group - 1)
        def _():
            pltpu.make_async_remote_copy(
                fsend.at[start + 3], frecv_extra.at[tm], f_sem.at[2], f_sem.at[3],
                device_id={"tm": to}, device_id_type=MESH,
            ).start()

    own_start = first_position(tm)
    pltpu.make_async_copy(fsend.at[pl.ds(own_start, 3)], frecv.at[tm], f_sem.at[1]).start()

    @pl.when(last)
    def _():
        pltpu.make_async_copy(fsend.at[own_start + 3], frecv_extra.at[tm], f_sem.at[3]).start()

    row = iota((rows, 2 * quarter), 0)
    column = iota((rows, 2 * quarter), 1)
    place = lax.rem(row, half)
    order = ((place < quarter) & (column == 2 * place + row // half)).astype(BF16)
    own_video = dot(order, vid[pl.ds(hx * quarter, quarter)].reshape(2 * quarter, model))

    for copy in out_x:
        copy.wait_recv()
    out_y = [
        send(out_block(0, 0), oy_sem, 0, ways[0]),
        send(out_block(0, 1), oy_sem, 1, ways[1]),
        send(out_block(0, 1), oy_sem, 2, ways[0]),
        send(out_block(0, 0), oy_sem, 3, ways[1]),
    ]
    out_y[0].wait_recv()
    out_y.append(send(out_block(3, 0), oy_sem, 4, ways[0]))
    out_y[1].wait_recv()
    out_y.append(send(out_block(1, 1), oy_sem, 5, ways[1]))
    for copy in mlp_x[:3]:
        copy.wait_recv()
    mlp_yz = [send(mlp_block(0, 0, third), y_sem, 8 + i, ways[i]) for i in range(2)]

    pltpu.make_async_copy(frecv, frecv, f_sem.at[1]).wait()

    def temporal(block):
        parts = []
        for head in range(heads):
            at = head * HD
            parts.append(
                attend(
                    block[:, at : at + HD],
                    block[:, width + at : width + at + HD],
                    block[:, 2 * width + at : 2 * width + at + HD],
                    None,
                )
            )
        mixed = jnp.concatenate(parts, axis=1).astype(BF16)
        return mixed.reshape(count, 2, width)

    for p in range(3):
        rsend[:, p] = temporal(frecv[:, p].reshape(2 * count, 3 * width))

    @pl.when(last)
    def _():
        pltpu.make_async_copy(frecv_extra, frecv_extra, f_sem.at[3]).wait()
        rsend_extra[...] = temporal(frecv_extra[...].reshape(2 * count, 3 * width))

    def send_back(to, local):
        pieces = [(rsend.at[to], rrecv.at[hx, pl.ds(3 * rank, 3)], 0, 1)]
        extra = (rsend_extra.at[to], rrecv.at[hx, 3 * group], 2, 3)

        def go(source, target, send, recv):
            if local:
                pltpu.make_async_copy(source, target, r_sem.at[recv]).start()
            else:
                pltpu.make_async_remote_copy(
                    source, target, r_sem.at[send], r_sem.at[recv],
                    device_id={"tm": to, "heads": home}, device_id_type=MESH,
                ).start()

        go(*pieces[0])

        @pl.when(last)
        def _():
            go(*extra)

    @pl.loop(0, count - 1)
    def _(k):
        send_back(other(k), False)

    @pl.when(home == hx)
    def _():
        send_back(tm, True)

    @pl.when(home != hx)
    def _():
        send_back(tm, False)

    for copy in out_y[2:]:
        copy.wait_recv()
    half_out = w_out.shape[1] // 2
    rows_out = pl.ds(pl.multiple_of(core * half_out, 16), half_out)
    out_given = send(w_out.at[others, rows_out], c_sem, 0, sibling)
    for copy in mlp_x[3:]:
        copy.wait_recv()

    pltpu.make_async_copy(
        fsend.at[pl.ds(0, 3 * (count - 1))], fsend.at[pl.ds(0, 3 * (count - 1))], f_sem.at[0]
    ).wait()

    @pl.when(last)
    def _():
        part = fsend.at[pl.ds(0, wide - 1)]
        pltpu.make_async_copy(part, part, f_sem.at[2]).wait()

    @pl.when(jnp.logical_not(last))
    def _():
        part = fsend.at[pl.ds(0, wide)]
        pltpu.make_async_copy(part, part, f_sem.at[2]).wait()

    most = rrecv.at[:, pl.ds(0, 3 * group)]
    pltpu.make_async_copy(most, most, r_sem.at[1]).wait()
    rest = rrecv.at[:, 3 * group]
    pltpu.make_async_copy(rest, rest, r_sem.at[3]).wait()
    mlp_yz += [
        send(mlp_block(0, (1 + i // 2) * third, third), y_sem, i, ways[i]) for i in range(4)
    ]
    part = mlp_share // 4
    given = [send(mlp_block(0, 0, mlp_share), c_sem, 1, sibling)]
    out_given.wait_recv()
    total = own_video
    for slot in range(wide):
        mixed = dot(order, rrecv[peer(slot)].reshape(2 * quarter, width)).astype(BF16)
        total += dot(mixed, w_out[slot, 0:width])
    x1 = total.astype(BF16).astype(F32)

    hbuf[hx] = layer_norm(x1, s_gain[...])
    upper, lower = pl.ds(0, rows // 32 * 16), pl.ds(rows // 32 * 16, rows - rows // 32 * 16)

    def pass_on(whose, part, i, step):
        block = hbuf.at[whose, part]
        copy = remote(block, block, h_sem, i, heads=peer(step))
        copy.start()
        return copy

    copies = [
        pass_on(hx, upper, 0, 1),
        pass_on(hx, lower, 1, 3),
        pass_on(hx, lower, 2, 1),
        pass_on(hx, upper, 3, 3),
    ]
    loads[6].wait()
    for step in (0, 1, 3, 2):
        if step == 2:
            for copy in mlp_yz:
                copy.wait_recv()
            onward = ((3, 1), (1, 0), (3, 3), (1, 2))
            for i, (whose, place) in enumerate(onward):
                block = mlp_block(whose, place * part, part)
                mlp_yz.append(send(block, y_sem, 4 + i, ways[i]))
            given.append(send(mlp_block(3, 0, mlp_share), c_sem, 2, sibling))
            given.append(send(mlp_block(1, 0, mlp_share), c_sem, 3, sibling))
        if step == 1:
            copies[0].wait_recv()
            copies.append(pass_on(peer(3), upper, 4, 1))
            copies[1].wait_recv()
            copies.append(pass_on(peer(1), lower, 5, 3))
        for i in ((), (2,), (4, 5), (3,))[step]:
            copies[i].wait_recv()
        at = peer(wide - step)
        projected = dot_t(hbuf[at], w_sqkv[...].reshape(3 * width, model))
        for f in range(2):
            sqkv[f, at] = projected[f * half : (f + 1) * half]
    keep = lax.rem(iota((1, wide * half), 1), half) < quarter
    for f in range(2):
        block = sqkv[f].reshape(wide * half, 3 * width).astype(BF16)
        for head in range(heads):
            at = head * HD
            smix[:, f, :, at : at + HD] = attend(
                block[:, at : at + HD],
                block[:, width + at : width + at + HD],
                block[:, 2 * width + at : 2 * width + at + HD],
                keep,
            ).reshape(wide, half, HD)
    mix_send[...] = smix[...].reshape(wide, rows, width).astype(BF16)
    mix_copies = []
    for step in (2, 1, 3):
        copy = remote(mix_send.at[peer(step)], mix_recv.at[hx], x_sem, step, heads=peer(step))
        copy.start()
        mix_copies.append(copy)
    for copy in mlp_yz[6:]:
        copy.wait_recv()
    given.append(send(mlp_block(2, 0, mlp_share), c_sem, 4, sibling))
    total = x1 + dot(mix_send[hx], w_out[0, width:])
    for step, copy in zip((2, 1, 3), mix_copies):
        copy.wait_recv()
        total += dot(mix_recv[peer(wide - step)], w_out[wide - step, width:])
    x2 = total.astype(BF16).astype(F32)

    normed = layer_norm(x2, m_gain[...])
    total = x2
    for slot in range(wide):
        if slot == 1:
            for copy in given:
                copy.wait_recv()
        up = dot(normed, w_mlp[slot, 0:model])
        shown = (0.5 * up * (1.0 + lax.erf(up * (0.5 ** 0.5)))).astype(BF16)
        total += dot(shown, w_mlp[slot, model:])
    for f in range(2):
        block_out[:, f] = total[f * half : f * half + quarter].astype(BF16)
    first = total[:half].astype(BF16)
    second = total[half:].astype(BF16)

    edge_send[0:half] = second
    edge_send[half:] = jnp.zeros((edge_send.shape[0] - half, model), BF16)
    to_next = pltpu.make_async_remote_copy(
        edge_send, edge_recv, e_sem.at[0], e_sem.at[1],
        device_id={"tm": lax.rem(tm + 1, count)}, device_id_type=MESH,
    )

    @pl.when(tm < count - 1)
    def _():
        to_next.start()

    loads[7].wait()
    result = dot(first, w_merge[1]) + dot(second, w_merge[2])

    @pl.when(tm > 0)
    def _():
        to_next.wait_recv()

    @pl.when(tm == 0)
    def _():
        edge_recv[...] = jnp.zeros_like(edge_recv)

    result += dot(edge_recv[0:half], w_merge[0])
    merged[0] = result[:quarter].astype(BF16)

    @pl.when(tm < count - 1)
    def _():
        to_next.wait_send()

    @pl.when(home == hx)
    def _():
        part = rsend.at[pl.ds(0, count - 1)]
        pltpu.make_async_copy(part, part, r_sem.at[0]).wait()

        @pl.when(last)
        def _():
            part = rsend_extra.at[pl.ds(0, count - 1)]
            pltpu.make_async_copy(part, part, r_sem.at[2]).wait()

    @pl.when(home != hx)
    def _():
        pltpu.make_async_copy(rsend, rsend, r_sem.at[0]).wait()

        @pl.when(last)
        def _():
            pltpu.make_async_copy(rsend_extra, rsend_extra, r_sem.at[2]).wait()

    for copy in (
        *copies, *mix_copies, *out_x, *out_y, *mlp_x, *mlp_yz, *given, out_given,
    ):
        copy.wait_send()


def local(video, t_gain, t_qkv, t_out, s_gain, s_qkv, s_out, m_gain, m_up, m_down, m_merge):
    count = lax.axis_size("tm")
    wide = lax.axis_size("heads")
    frames, positions, model = video.shape
    width = t_qkv.shape[1]
    hidden = m_up.shape[1]
    quarter = positions // wide
    half = -(-quarter // 8) * 8
    rows = 2 * half
    edge = -(-half // 16) * 16
    vmem = pltpu.VMEM
    dma = pltpu.SemaphoreType.DMA
    in_vmem = pl.BlockSpec(memory_space=pltpu.VMEM)
    anywhere = pl.BlockSpec(memory_space=pl.ANY)
    out, together = pl.pallas_call(
        kernel,
        out_shape=(
            jax.ShapeDtypeStruct((quarter, frames, model), BF16),
            jax.ShapeDtypeStruct((frames // 2, quarter, model), BF16),
        ),
        in_specs=[
            anywhere, in_vmem, anywhere, anywhere, in_vmem, anywhere, anywhere, in_vmem,
            anywhere, anywhere, anywhere,
        ],
        out_specs=(in_vmem, in_vmem),
        scratch_shapes=[
            vmem((positions, frames, model), BF16),
            vmem((3, width, model), BF16),
            vmem((wide, 2 * width, model), BF16),
            vmem((3, width, model), BF16),
            vmem((wide, model + hidden, model), BF16),
            vmem((3, model, model), BF16),
            vmem((positions, 2, 3 * width), BF16),
            vmem((count, 3, 2, 3 * width), BF16),
            vmem((count, 2, 3 * width), BF16),
            vmem((count, 3, 2, width), BF16),
            vmem((count, 2, width), BF16),
            vmem((wide, quarter, 2, width), BF16),
            vmem((wide, rows, model), BF16),
            vmem((2, wide, half, 3 * width), F32),
            vmem((wide, 2, half, width), F32),
            vmem((wide, rows, width), BF16),
            vmem((wide, rows, width), BF16),
            vmem((edge, model), BF16),
            vmem((edge, model), BF16),
            dma((8,)), dma((2, 4)), dma((2, 6)), dma((2, 8)), dma((2, 10)), dma((2, 5)),
            dma((4,)), dma((4,)), dma((2, 6)), dma((2, 4)), dma((2,)),
        ],
        compiler_params=pltpu.CompilerParams(
            collective_id=0, has_side_effects=True, vmem_limit_bytes=107 * 2**19
        ),
    )(
        jnp.swapaxes(video, 0, 1), t_gain, t_qkv, t_out, s_gain, s_qkv, s_out, m_gain,
        m_up, m_down, m_merge,
    )
    return jnp.swapaxes(out, 0, 1), together


def solution(mesh):
    placed = (
        P("tm", None, None),
        P(),
        P(None, "heads", None),
        P("heads", None),
        P(),
        P(None, "heads", None),
        P("heads", None),
        P(),
        P(None, "heads"),
        P("heads", None),
        P(),
    )
    return jax.shard_map(
        local,
        mesh=mesh,
        in_specs=placed,
        out_specs=(P("tm", "heads", None), P("tm", "heads", None)),
        check_vma=False,
    )
```
